32 devices in a mesh: ang: 8 (over y, x, core), row: 4 (over z).
Axes of the slice: x: 2, y: 2, z: 4, core: 2. Of those that a mesh axis runs over, the one named last changes fastest.
Arguments:
- sinogram: float32 [256, 8, 4096], P('ang', 'row'), may hold values from -3 to 16
- col_weights: bfloat16 [32, 256, 128], replicated
- col_start: int32 [32], replicated, may hold values from 0 to 3840, as said below
- view_offset: int32 [32], replicated, may hold values from -32 to 29, as said below
- row_offset: int32 [32], replicated, may hold values from -2 to 1, as said below
- conj_offset: int32 [32], replicated, may hold values from -16 to 16, as said below
- ang_weights: float32 [4, 4096], replicated, may hold values from -0.5 to 1
- row_weights: float32 [2, 4096], replicated, may hold values from 0 to 1
Outputs:
- filtered: float32 [256, 8, 8192], P('ang', 'row')
The draws below stay inside these ranges and needn't reach their ends.
Inputs may be any that keep to these rules, and one draw needn't show every extreme that they name: `col_start`: both ends are taken by some column tile in every draw. `view_offset`: both ends are taken by some column tile in every draw. `row_offset`: both ends are taken by some column tile in every draw. `conj_offset`: both ends are taken by some column tile in every draw.
All inputs are finite; a program needn't handle non-finite values.
Results may differ from the reference program's by a relative error of at most 0.0003.
Values sent between devices are 32-bit elements; how exact they have to be, the bound alone decides.
No kernel may reach another device: no remote copies, remote signals or barrier semaphores. Data moves between devices by JAX's collectives and lax.ppermute only.
A program may use at most 64 MiB of HBM per device.

```python
import math
import jax
import jax.numpy as jnp
from jax import lax

COLS = 4096
TILE = 128
COL_TILES = 32
BAND = 256
TAPS = 4
KR = 256
VIEW_DEV = 32
ROW_DEV = 2
VIEWS = 256
ROWS = 8


def forced_ends(key, number, lowest, highest):
    key_values, key_placing = jax.random.split(key)
    values = jax.random.randint(key_values, (number,), lowest, highest + 1)
    placing = jax.random.permutation(key_placing, number)
    values = values.at[placing[0]].set(lowest)
    values = values.at[placing[1]].set(highest)
    return values.astype(jnp.int32)


def draw_sinogram(key, part):
    subkeys = jax.random.split(jax.random.fold_in(key, 53), 10)
    position = (jnp.arange(COLS, dtype=jnp.float32) + 0.5) / COLS
    position = position[None, None, :]
    lowest_height = 3.0
    highest_height = 8.0
    smooth = jnp.zeros((VIEWS, ROWS, COLS), jnp.float32)
    for profile_index in range(3):
        centre = jax.random.uniform(subkeys[3 * profile_index], (VIEWS, ROWS, 1), jnp.float32, 0.1, 0.9)
        spread = jax.random.uniform(subkeys[3 * profile_index + 1], (VIEWS, ROWS, 1), jnp.float32, 0.15, 0.35)
        height = jax.random.uniform(subkeys[3 * profile_index + 2], (VIEWS, ROWS, 1), jnp.float32, lowest_height, highest_height)
        smooth = smooth + height * jnp.exp(-((position - centre) / spread) ** 2)
    jitter = jax.random.normal(subkeys[9], (VIEWS, ROWS, COLS), jnp.float32)
    return jnp.clip(smooth + jitter, -3.0, 16.0).astype(jnp.float32)


def draw_col_weights(key, part):
    key_factor, key_offset = jax.random.split(jax.random.fold_in(key, 61))
    stretch = BAND / TILE
    breadth = 1.0 + stretch
    offsets = jax.random.uniform(key_offset, (COL_TILES, 1, 1), jnp.float32, 0.0, stretch)
    band_place = jnp.arange(BAND, dtype=jnp.float32)[None, :, None]
    out_place = jnp.arange(TILE, dtype=jnp.float32)[None, None, :]
    profile = jnp.exp(-((band_place - out_place * stretch - offsets) / breadth) ** 2)
    factor = jax.random.uniform(key_factor, (COL_TILES, BAND, TILE), jnp.float32, 0.5, 1.5)
    values = factor * (profile / (breadth * math.sqrt(math.pi)) + 0.25 / BAND)
    return values.astype(jnp.bfloat16)


def draw_col_start(key, part):
    return forced_ends(jax.random.fold_in(key, 11), COL_TILES, 0, COLS - BAND)


def draw_view_offset(key, part):
    return forced_ends(jax.random.fold_in(key, 23), COL_TILES, -VIEW_DEV, VIEW_DEV - TAPS + 1)


def draw_row_offset(key, part):
    return forced_ends(jax.random.fold_in(key, 37), COL_TILES, -ROW_DEV, ROW_DEV - 1)


def draw_conj_offset(key, part):
    return forced_ends(jax.random.fold_in(key, 41), COL_TILES, -(VIEW_DEV // 2), VIEW_DEV // 2)


def setup_inputs(seed: int = 0) -> dict:
    streams_of = jax.random.split(jax.random.key(seed), 9)
    return {
        "sinogram": draw_sinogram(jax.random.fold_in(streams_of[8], 71), 0),
        "col_weights": draw_col_weights(jax.random.fold_in(streams_of[8], 71), 0),
        "col_start": draw_col_start(jax.random.fold_in(streams_of[8], 71), 0),
        "view_offset": draw_view_offset(jax.random.fold_in(streams_of[8], 71), 0),
        "row_offset": draw_row_offset(jax.random.fold_in(streams_of[8], 71), 0),
        "conj_offset": draw_conj_offset(jax.random.fold_in(streams_of[8], 71), 0),
        "ang_weights": jnp.clip(jax.random.uniform(streams_of[6], (TAPS, COLS), jnp.float32, -0.5, 1.0), -0.5, 1.0),
        "row_weights": jnp.clip(jax.random.uniform(streams_of[7], (2, COLS), jnp.float32, 0.0, 1.0), 0.0, 1.0),
    }


def ramp_kernel(lag, reach):
    lag_float = lag.astype(jnp.float32)
    odd_lag = (lag % 2) != 0
    inverse = -1.0 / (math.pi * math.pi * jnp.maximum(lag_float * lag_float, 1.0))
    values = jnp.where(lag == 0, 0.25, jnp.where(odd_lag, inverse, 0.0))
    values = jnp.where(jnp.abs(lag) <= reach, values, 0.0)
    return values.astype(jnp.float32)


def tile_major_to_columns(tiles_major):
    return jnp.transpose(tiles_major, (1, 2, 0, 3)).reshape(tiles_major.shape[1], tiles_major.shape[2], -1)


def reference(sinogram, col_weights, col_start, view_offset, row_offset, conj_offset, ang_weights, row_weights):
    tile_numbers = jnp.arange(COL_TILES, dtype=jnp.int32)

    def rebin_tile(tile_index):
        slab = lax.dynamic_slice_in_dim(sinogram, col_start[tile_index].astype(jnp.int32), BAND, axis=2)
        weights = col_weights[tile_index].astype(jnp.float32)
        resampled = jnp.einsum("vrb,bc->vrc", slab, weights, precision=lax.Precision.HIGHEST)
        padded = jnp.pad(resampled, ((0, 0), (ROWS, ROWS), (0, 0)))
        first_col = (tile_index * TILE).astype(jnp.int32)
        row_pair = lax.dynamic_slice_in_dim(row_weights, first_col, TILE, axis=1)
        row_start = (ROWS + row_offset[tile_index]).astype(jnp.int32)
        lower = lax.dynamic_slice_in_dim(padded, row_start, ROWS, axis=1)
        upper = lax.dynamic_slice_in_dim(padded, row_start + 1, ROWS, axis=1)
        rowed = row_pair[0] * lower + row_pair[1] * upper
        angle_pair = lax.dynamic_slice_in_dim(ang_weights, first_col, TILE, axis=1)
        angular = jnp.zeros(rowed.shape, jnp.float32)
        for angle_tap in range(TAPS):
            rolled = jnp.roll(rowed, -(view_offset[tile_index] + angle_tap), axis=0)
            angular = angular + angle_pair[angle_tap] * rolled
        return angular

    par_tiles = lax.map(rebin_tile, tile_numbers)

    def conj_tile(tile_index):
        source = par_tiles[COL_TILES - 1 - tile_index][:, :, ::-1]
        return jnp.roll(source, -(VIEWS // 2 + conj_offset[tile_index]), axis=0)

    conj_tiles = lax.map(conj_tile, tile_numbers)
    parallel = tile_major_to_columns(par_tiles)
    conjugate = tile_major_to_columns(conj_tiles)
    margin = ((0, 0), (0, 0), (KR // 2, KR // 2))
    par_pad = jnp.pad(parallel, margin)
    conj_pad = jnp.pad(conjugate, margin)
    lag = jnp.arange(2 * TILE, dtype=jnp.int32)[None, :] - 2 * jnp.arange(TILE + KR, dtype=jnp.int32)[:, None] + KR
    kernel_even = ramp_kernel(lag, KR)
    kernel_odd = ramp_kernel(lag - 1, KR)

    def filter_tile(tile_index):
        start = (tile_index * TILE).astype(jnp.int32)
        par_slab = lax.dynamic_slice_in_dim(par_pad, start, TILE + KR, axis=2)
        conj_slab = lax.dynamic_slice_in_dim(conj_pad, start, TILE + KR, axis=2)
        total = jnp.einsum("vri,ib->vrb", par_slab, kernel_even, precision=lax.Precision.HIGHEST)
        total = total + jnp.einsum("vri,ib->vrb", conj_slab, kernel_odd, precision=lax.Precision.HIGHEST)
        return total

    out_tiles = lax.map(filter_tile, tile_numbers)
    return tile_major_to_columns(out_tiles)
```

```python
import functools
import math

import jax
import jax.numpy as jnp
import numpy as np
from jax import lax
from jax.experimental import pallas as pl
from jax.experimental.pallas import tpu as pltpu
from jax.sharding import PartitionSpec as P

KR = 256
LANES = 128
WINDOW = 3 * LANES
WRAP = 72
VMEM = pl.BlockSpec(memory_space=pltpu.VMEM)
SMEM = pl.BlockSpec(memory_space=pltpu.SMEM)
PARAMS = pltpu.CompilerParams(vmem_limit_bytes=48 * 1024 * 1024)


def call(body, outs, scratch, args, flops, moved):
    smem = [a.dtype == jnp.int32 for a in args]
    return pl.pallas_call(
        body,
        out_shape=outs,
        in_specs=[SMEM if s else VMEM for s in smem],
        out_specs=[VMEM] * len(outs),
        scratch_shapes=scratch,
        compiler_params=PARAMS,
        cost_estimate=pl.CostEstimate(flops=flops, bytes_accessed=moved, transcendentals=0),
    )(*args)


def f32(*shape):
    return jax.ShapeDtypeStruct(shape, jnp.float32)


def tile_of(index, group, tiles):
    first, half = group
    return jnp.where(index < half, first + index, tiles - first - 2 * half + index)


def split(x):
    high = x.astype(jnp.bfloat16)
    low = (x - high.astype(jnp.float32)).astype(jnp.bfloat16)
    return high, low


def dot(a, b):
    return jnp.dot(a, b, preferred_element_type=jnp.float32)


def resample_body(group, start_ref, sino_ref, weights_ref, out_ref):
    tiles, band, _ = weights_ref.shape
    views, rows, cols = sino_ref.shape

    def step(index, carry):
        tile = tile_of(index, group, tiles)
        start = start_ref[tile]
        base = jnp.minimum(start // LANES * LANES, cols - WINDOW)
        shift = start - base
        slab = sino_ref[:, :, pl.ds(pl.multiple_of(base, LANES), WINDOW)]
        slab = slab.reshape(views * rows, WINDOW)
        slab = pltpu.roll(slab, WINDOW - shift, 1)[:, :band]
        high, low = split(slab)
        weights = weights_ref[tile]
        out_ref[index] = dot(high, weights) + dot(low, weights)
        return carry

    lax.fori_loop(0, 2 * group[1], step, 0, unroll=2)


def resample(group, start, sino, weights):
    views, rows, cols = sino.shape
    count = 2 * group[1]
    flops = 4 * count * views * rows * weights.shape[1] * LANES
    return call(
        functools.partial(resample_body, group),
        [f32(count, views * rows, LANES)],
        [],
        (start, sino, weights),
        flops,
        6 << 20,
    )[0]


def rows_body(group, tiles, offset_ref, prev_ref, own_ref, next_ref, weights_ref, keep_ref, send_ref, stack):
    count, height, _ = own_ref.shape
    views = height // 2
    core = lax.axis_index("ang") % 2

    def step(index, slot):
        tile = tile_of(index, group, tiles)
        offset = offset_ref[tile]
        stack[slot, 0:height] = prev_ref[index]
        stack[slot, height : 2 * height] = own_ref[index]
        stack[slot, 2 * height : 3 * height] = next_ref[index]
        weights = weights_ref[:, pl.ds(pl.multiple_of(tile * LANES, LANES), LANES)]

        def picked(row):
            lifted = row + 2
            first = lifted // 2 * height + lifted % 2
            return stack[slot, pl.ds(first, views, stride=2), :]

        for out_ref, row in ((keep_ref, core), (send_ref, 1 - core)):
            lower = picked(row + offset)
            upper = picked(row + offset + 1)
            out_ref[index] = weights[0:1] * lower + weights[1:2] * upper

    def pair(index, carry):
        step(2 * index, 0)
        step(2 * index + 1, 1)
        return carry

    lax.fori_loop(0, count // 2, pair, 0)


def interpolate_rows(group, tiles, offset, prev, own, after, weights):
    count, height, _ = own.shape
    return call(
        functools.partial(rows_body, group, tiles),
        [f32(count, height // 2, LANES)] * 2,
        [pltpu.VMEM((2, 3 * height, LANES), jnp.float32)],
        (offset, prev, own, after, weights),
        count * height * LANES * 4,
        count * height * LANES * 16,
    )


def views_body(group, tiles, chips, places, view_ref, conj_ref, weights_ref, *refs):
    blocks = refs[: len(places)]
    keep_ref, send_ref, stack = refs[len(places) :]
    count, chip_views = keep_ref.shape[0], 2 * keep_ref.shape[2]
    views = chip_views // 2
    turn = chips * chip_views
    index_ang = lax.axis_index("ang")
    chip, core = index_ang // 2, index_ang % 2
    taps = weights_ref.shape[0]

    def step(index, slot):
        tile = tile_of(index, group, tiles)
        for ref, (place, low, high) in zip(blocks, places):

            def put(ref=ref, place=place, low=low):
                at = place(chip) * chip_views
                mine = pl.multiple_of(at + core * views, 8)
                other = pl.multiple_of(at + (1 - core) * views, 8)
                stack[slot, pl.ds(mine, views)] = ref[index - low, 0:views]
                stack[slot, pl.ds(other, views)] = ref[index - low, views:chip_views]

            if low == 0 and high == count:
                put()
            else:
                pl.when((index >= low) & (index < high))(put)
        stack[slot, turn : turn + WRAP] = stack[slot, 0:WRAP]
        weights = weights_ref[:, pl.ds(pl.multiple_of(tile * LANES, LANES), LANES)]
        shift = view_ref[tile]
        opposite = shift + conj_ref[tiles - 1 - tile] + turn // 2
        for part, by in ((0, shift), (1, opposite)):
            for out_ref, first in ((keep_ref, core), (send_ref, 1 - core)):
                begin = lax.rem(chip * chip_views + first * views + by + turn, turn)
                total = weights[0:1] * stack[slot, pl.ds(begin, views)]
                for tap in range(1, taps):
                    total = total + weights[tap : tap + 1] * stack[slot, pl.ds(begin + tap, views)]
                out_ref[index, part] = total

    def pair(index, carry):
        step(2 * index, 0)
        step(2 * index + 1, 1)
        return carry

    lax.fori_loop(0, count // 2, pair, 0)


def interpolate_views(group, tiles, chips, view_offset, conj_offset, weights, blocks):
    places = tuple(place for _, place in blocks)
    arrays = [array for array, _ in blocks]
    count = 2 * group[1]
    views = arrays[0].shape[1] // 2
    return call(
        functools.partial(views_body, group, tiles, chips, places),
        [f32(count, 2, views, LANES)] * 2,
        [pltpu.VMEM((2, chips * 2 * views + WRAP, LANES), jnp.float32)],
        (view_offset, conj_offset, weights, *arrays),
        count * views * LANES * 32,
        count * views * LANES * 64,
    )


def ramp(lag):
    lag = lag.astype(np.float64)
    odd = np.abs(lag) % 2 == 1
    values = np.where(lag == 0, 0.25, np.where(odd, -1.0 / (math.pi**2 * np.maximum(lag * lag, 1.0)), 0.0))
    return np.where(np.abs(lag) <= KR, values, 0.0).astype(np.float32)


def filter_matrix():
    column = np.arange(WINDOW)[:, None]
    place = np.arange(2 * LANES)[None, :]
    lag = place - 2 * (column - LANES)
    even = ramp(lag)
    odd = ramp(lag - 1)[::-1]
    whole = jnp.asarray(np.concatenate([even, odd], axis=0))
    return split(whole)


def filter_body(groups, tiles, high_ref, low_ref, *refs):
    number = len(groups)
    keeps, gots = refs[:number], refs[number : 2 * number]
    out_ref, mixed, high_all, low_all = refs[2 * number :]
    views = out_ref.shape[0]
    core = lax.axis_index("ang") % 2
    for ref in (high_all, low_all):
        for part in range(2):
            ref[part, 0] = jnp.zeros(ref.shape[2:], ref.dtype)
            ref[part, tiles + 1] = jnp.zeros(ref.shape[2:], ref.dtype)
    for group, keep, got in zip(groups, keeps, gots):

        def gather(index, carry, group=group, keep=keep, got=got):
            tile = tile_of(index, group, tiles)
            for part in range(2):
                mixed[part, pl.ds(core, views, stride=2), :] = keep[index, part]
                mixed[part, pl.ds(1 - core, views, stride=2), :] = got[index, part]
                high, low = split(mixed[part])
                high_all[part, tile + 1] = high
                low_all[part, tile + 1] = low
            return carry

        lax.fori_loop(0, 2 * group[1], gather, 0, unroll=2)

    batch = 4

    def produce(index, carry):
        first = index * batch

        def window(ref):
            pieces = []
            for part in range(2):
                begin = first if part == 0 else tiles - first - batch
                for section in range(3):
                    if part == 0:
                        piece = ref[0, pl.ds(begin + section, batch)]
                    else:
                        piece = jnp.stack(
                            [ref[1, begin + section + batch - 1 - i] for i in range(batch)]
                        )
                    pieces.append(piece.reshape(batch * 2 * views, LANES))
            return jnp.concatenate(pieces, axis=1)

        high, low = window(high_all), window(low_all)
        total = dot(high, high_ref[...]) + dot(low, high_ref[...]) + dot(high, low_ref[...])
        for i in range(batch):
            block = total[2 * views * i : 2 * views * (i + 1)].reshape(views, 2, 2 * LANES)
            at = pl.multiple_of((first + i) * 2 * LANES, 2 * LANES)
            out_ref[:, :, pl.ds(at, 2 * LANES)] = block
        return carry

    lax.fori_loop(0, tiles // batch, produce, 0)


def ramp_filter(groups, tiles, keeps, gots):
    views = keeps[0].shape[2]
    high, low = filter_matrix()
    stored = pltpu.VMEM((2, tiles + 2, 2 * views, LANES), jnp.bfloat16)
    return call(
        functools.partial(filter_body, groups, tiles),
        [f32(views, 2, 2 * tiles * LANES)],
        [pltpu.VMEM((2, 2 * views, LANES), jnp.float32), stored, stored],
        (high, low, *keeps, *gots),
        6 * tiles * 2 * views * 2 * WINDOW * 2 * LANES,
        5 << 20,
    )[0]


def permuted(value, axis, target):
    count = lax.axis_size(axis)
    pairs = [(i, target(i)) for i in range(count)]
    return lax.ppermute(value, axis, [(i, j) for i, j in pairs if 0 <= j < count])


def chip_blocks(block):
    devices = lax.axis_size("ang")
    chips = devices // 2
    count = block.shape[0]
    if chips == 4:
        by_x = permuted(block, "ang", lambda i: i ^ 2)
        by_y = permuted(block, "ang", lambda i: i ^ 4)
        half = count // 2
        lower = permuted(by_x[:half], "ang", lambda i: i ^ 4)
        upper = permuted(by_y[half:], "ang", lambda i: i ^ 2)
        return [
            (block, (lambda p: p, 0, count)),
            (by_x, (lambda p: p ^ 1, 0, count)),
            (by_y, (lambda p: p ^ 2, 0, count)),
            (lower, (lambda p: p ^ 3, 0, half)),
            (upper, (lambda p: p ^ 3, half, count)),
        ]
    found = [(block, (lambda p: p, 0, count))]
    ahead = {d % chips for d in (-1, 1, chips // 2 - 1, chips // 2, chips // 2 + 1)} - {0}
    for steps in sorted(ahead):
        got = permuted(block, "ang", lambda i, steps=steps: (i - 2 * steps) % devices)
        found.append((got, (lambda p, steps=steps: lax.rem(p + steps, chips), 0, count)))
    return found


def on_device(
    sinogram, col_weights, col_start, view_offset, row_offset, conj_offset, ang_weights, row_weights
):
    tiles = col_weights.shape[0]
    chips = lax.axis_size("ang") // 2
    groups = ((0, tiles // 4), (tiles // 4, tiles // 4))
    keeps, gots = [], []
    for group in groups:
        own = resample(group, col_start, sinogram, col_weights)
        prev = permuted(own, "row", lambda i: i + 1)
        after = permuted(own, "row", lambda i: i - 1)
        keep, send = interpolate_rows(group, tiles, row_offset, prev, own, after, row_weights)
        got = permuted(send, "ang", lambda i: i ^ 1)
        block = jnp.concatenate([keep, got], axis=1)
        blocks = chip_blocks(block)
        keep, send = interpolate_views(
            group, tiles, chips, view_offset, conj_offset, ang_weights, blocks
        )
        keeps.append(keep)
        gots.append(permuted(send, "ang", lambda i: i ^ 1))
    return ramp_filter(groups, tiles, keeps, gots)


def solution(mesh):
    return jax.shard_map(
        on_device,
        mesh=mesh,
        in_specs=(P("ang", "row", None), P(), P(), P(), P(), P(), P(), P()),
        out_specs=P("ang", "row", None),
        check_vma=False,
    )
```

```python
import functools
import math

import jax
import jax.numpy as jnp
import numpy as np
from jax import lax
from jax.experimental import pallas as pl
from jax.experimental.pallas import tpu as pltpu
from jax.sharding import PartitionSpec as P

KR = 256
LANES = 128
WINDOW = 3 * LANES
VMEM = pl.BlockSpec(memory_space=pltpu.VMEM)
SMEM = pl.BlockSpec(memory_space=pltpu.SMEM)
PARAMS = pltpu.CompilerParams(vmem_limit_bytes=48 * 1024 * 1024)


def call(body, outs, scratch, args, flops, moved):
    smem = [a.dtype == jnp.int32 for a in args]
    return pl.pallas_call(
        body,
        out_shape=outs,
        in_specs=[SMEM if s else VMEM for s in smem],
        out_specs=[VMEM] * len(outs),
        scratch_shapes=scratch,
        compiler_params=PARAMS,
        cost_estimate=pl.CostEstimate(flops=flops, bytes_accessed=moved, transcendentals=0),
    )(*args)


def f32(*shape):
    return jax.ShapeDtypeStruct(shape, jnp.float32)


def tile_of(index, group, tiles):
    first, half = group
    return jnp.where(index < half, first + index, tiles - first - 2 * half + index)


def split(x):
    high = x.astype(jnp.bfloat16)
    low = (x - high.astype(jnp.float32)).astype(jnp.bfloat16)
    return high, low


def dot(a, b):
    return jnp.dot(a, b, preferred_element_type=jnp.float32)


def resample_body(group, start_ref, sino_ref, weights_ref, out_ref):
    tiles, band, _ = weights_ref.shape
    views, rows, cols = sino_ref.shape

    def step(index, carry):
        tile = tile_of(index, group, tiles)
        start = start_ref[tile]
        base = jnp.minimum(start // LANES * LANES, cols - WINDOW)
        shift = start - base
        slab = sino_ref[:, :, pl.ds(pl.multiple_of(base, LANES), WINDOW)]
        slab = slab.reshape(views * rows, WINDOW)
        slab = pltpu.roll(slab, WINDOW - shift, 1)[:, :band]
        high, low = split(slab)
        weights = weights_ref[tile]
        out_ref[index] = dot(high, weights) + dot(low, weights)
        return carry

    lax.fori_loop(0, 2 * group[1], step, 0, unroll=2)


def resample(group, start, sino, weights):
    views, rows, cols = sino.shape
    count = 2 * group[1]
    flops = 4 * count * views * rows * weights.shape[1] * LANES
    return call(
        functools.partial(resample_body, group),
        [f32(count, views * rows, LANES)],
        [],
        (start, sino, weights),
        flops,
        6 << 20,
    )[0]


def rows_body(group, tiles, offset_ref, prev_ref, own_ref, next_ref, weights_ref, keep_ref, send_ref, stack):
    count, height, _ = own_ref.shape
    views = height // 2
    core = lax.axis_index("ang") % 2

    def step(index, slot):
        tile = tile_of(index, group, tiles)
        offset = offset_ref[tile]
        stack[slot, 0:height] = prev_ref[index]
        stack[slot, height : 2 * height] = own_ref[index]
        stack[slot, 2 * height : 3 * height] = next_ref[index]
        weights = weights_ref[:, pl.ds(pl.multiple_of(tile * LANES, LANES), LANES)]

        def picked(row):
            lifted = row + 2
            first = lifted // 2 * height + lifted % 2
            return stack[slot, pl.ds(first, views, stride=2), :]

        for out_ref, row in ((keep_ref, core), (send_ref, 1 - core)):
            lower = picked(row + offset)
            upper = picked(row + offset + 1)
            mixed = weights[0:1] * lower + weights[1:2] * upper
            if out_ref is send_ref:
                out_ref[index] = mixed
            else:
                out_ref[index, pl.ds(pl.multiple_of(core * views, 8), views)] = mixed

    def pair(index, carry):
        step(2 * index, 0)
        step(2 * index + 1, 1)
        return carry

    lax.fori_loop(0, count // 2, pair, 0)


def interpolate_rows(group, tiles, offset, prev, own, after, weights):
    count, height, _ = own.shape
    return call(
        functools.partial(rows_body, group, tiles),
        [f32(count, height, LANES), f32(count, height // 2, LANES)],
        [pltpu.VMEM((2, 3 * height, LANES), jnp.float32)],
        (offset, prev, own, after, weights),
        count * height * LANES * 4,
        count * height * LANES * 16,
    )


def select_body(group, tiles, view_ref, conj_ref, own_ref, by_y_ref, by_x_ref, for_x_ref, for_y_ref, stack):
    half = group[1]
    chip_views = own_ref.shape[1]
    side = lax.axis_index("ang") // 2 % 2
    lanes = own_ref.shape[2]

    def shifts(index):
        tile = tile_of(index, group, tiles)
        shift = view_ref[tile]
        return shift, shift + conj_ref[tiles - 1 - tile]

    def slots(low, high):
        return low + lax.broadcasted_iota(jnp.int32, (high - low, lanes), 0)

    def across_x(index, slot):
        shift, opposite = shifts(index)
        own_at = pl.multiple_of((1 - side) * chip_views, 8)
        got_at = pl.multiple_of(side * chip_views, 8)
        stack[slot, pl.ds(own_at, chip_views)] = own_ref[index]
        stack[slot, pl.ds(got_at, chip_views)] = by_y_ref[index]
        near, far = stack.at[slot, 0:64], stack.at[slot, 64:128]
        for_x_ref[index, 0:32] = jnp.where(slots(0, 32) >= shift + 32, far[32:64], near[0:32])
        for_x_ref[index, 32:80] = jnp.where(slots(0, 48) >= opposite + 48, near[16:64], far[0:48])

    def across_y_first(index, slot):
        shift, opposite = shifts(half + index)
        stack[slot, 0:64] = own_ref[half + index]
        stack[slot, 64:128] = by_x_ref[index]
        both = stack.at[slot]
        for_y_ref[index, 0:40] = jnp.where(slots(0, 40) >= opposite, both[0:40], both[72:112])
        for_y_ref[index, 40:56] = both[40:56]
        for_y_ref[index, 56:72] = jnp.where(slots(56, 72) >= 88 + shift, both[96:112], both[56:72])
        for_y_ref[index, 72:88] = both[112:128]

    def across_y_last(index, slot):
        shift, opposite = shifts(half + index)
        stack[slot, 0:64] = by_x_ref[index]
        stack[slot, 64:128] = own_ref[half + index]
        both = stack.at[slot]
        for_y_ref[index, 0:16] = both[0:16]
        for_y_ref[index, 16:32] = jnp.where(slots(16, 32) < shift + 3, both[16:32], both[56:72])
        for_y_ref[index, 32:48] = both[72:88]
        for_y_ref[index, 48:88] = jnp.where(slots(48, 88) < 91 + opposite, both[88:128], both[16:56])

    paired(across_x, half)
    pl.when(side == 0)(lambda: paired(across_y_first, half))
    pl.when(side == 1)(lambda: paired(across_y_last, half))


def paired(step, count):
    def pair(index, carry):
        step(2 * index, 0)
        step(2 * index + 1, 1)
        return carry

    lax.fori_loop(0, count // 2, pair, 0)


def select_views(group, tiles, view_offset, conj_offset, own, by_y, by_x):
    half = group[1]
    return call(
        functools.partial(select_body, group, tiles),
        [f32(half, 80, LANES), f32(half, 88, LANES)],
        [pltpu.VMEM((2, 128, LANES), jnp.float32)],
        (view_offset, conj_offset, own, by_y, by_x),
        half * LANES * 1000,
        half * LANES * 2000,
    )


def views_body(group, tiles, exchanged, view_ref, conj_ref, weights_ref, *refs):
    *blocks, keep_ref, send_ref, stack = refs
    half = group[1]
    views = keep_ref.shape[2]
    index_ang = lax.axis_index("ang")
    side, core = index_ang // 2 % 2, index_ang % 2
    taps = weights_ref.shape[0]

    def interpolate(index, slot):
        tile = tile_of(index, group, tiles)
        weights = weights_ref[:, pl.ds(pl.multiple_of(tile * LANES, LANES), LANES)]
        shift = view_ref[tile]
        opposite = shift + conj_ref[tiles - 1 - tile]
        for part, by in ((0, 32 + shift), (1, 176 + opposite)):
            for out_ref, first in ((keep_ref, core), (send_ref, 1 - core)):
                begin = by + first * views
                total = weights[0:1] * stack[slot, pl.ds(begin, views)]
                for tap in range(1, taps):
                    total = total + weights[tap : tap + 1] * stack[slot, pl.ds(begin + tap, views)]
                out_ref[index, part] = total

    def filled(slot, *parts):
        at = 0
        for part in parts:
            stack[slot, at : at + part.shape[0]] = part[...]
            at += part.shape[0]

    if not exchanged:
        own, before, after, early, middle, late = blocks

        def whole(index, slot):
            parts = (before, own, after, early, middle, late)
            filled(slot, *(ref.at[index] for ref in parts))
            interpolate(index, slot)

        paired(whole, 2 * half)
        return
    own, by_y, by_x, from_x, from_y = blocks

    def first_half(index, slot):
        near, far = from_x.at[index, 0:32], from_x.at[index, 32:80]
        filled(slot, near, own.at[index], near, far, by_y.at[index], far)
        interpolate(index, slot)

    def last_half_first(index, slot):
        got = from_y.at[index]
        beside = by_x.at[index]
        filled(
            slot, got.at[56:88], own.at[half + index], beside.at[0:32], beside.at[16:64], got.at[0:72], got.at[0:40]
        )
        interpolate(half + index, slot)

    def last_half_last(index, slot):
        got = from_y.at[index]
        beside = by_x.at[index]
        filled(
            slot, beside.at[32:64], own.at[half + index], got.at[0:32], got.at[48:88], got.at[16:88], beside.at[0:48]
        )
        interpolate(half + index, slot)

    paired(first_half, half)
    pl.when(side == 0)(lambda: paired(last_half_first, half))
    pl.when(side == 1)(lambda: paired(last_half_last, half))


def interpolate_views(group, tiles, exchanged, view_offset, conj_offset, weights, blocks):
    count = 2 * group[1]
    views = blocks[0].shape[1] // 2
    return call(
        functools.partial(views_body, group, tiles, exchanged),
        [f32(count, 2, views, LANES)] * 2,
        [pltpu.VMEM((2, 288, LANES), jnp.float32)],
        (view_offset, conj_offset, weights, *blocks),
        count * views * LANES * 32,
        count * views * LANES * 64,
    )


def ramp(lag):
    lag = lag.astype(np.float64)
    odd = np.abs(lag) % 2 == 1
    values = np.where(lag == 0, 0.25, np.where(odd, -1.0 / (math.pi**2 * np.maximum(lag * lag, 1.0)), 0.0))
    return np.where(np.abs(lag) <= KR, values, 0.0).astype(np.float32)


def filter_matrix():
    column = np.arange(WINDOW)[:, None]
    place = np.arange(2 * LANES)[None, :]
    lag = place - 2 * (column - LANES)
    even = ramp(lag)
    odd = ramp(lag - 1)[::-1]
    whole = jnp.asarray(np.concatenate([even, odd], axis=0))
    return split(whole)


def filter_body(groups, tiles, high_ref, low_ref, *refs):
    number = len(groups)
    keeps, gots = refs[:number], refs[number : 2 * number]
    out_ref, mixed, high_all, low_all = refs[2 * number :]
    views = out_ref.shape[0]
    core = lax.axis_index("ang") % 2
    for ref in (high_all, low_all):
        for part in range(2):
            ref[part, 0] = jnp.zeros(ref.shape[2:], ref.dtype)
            ref[part, tiles + 1] = jnp.zeros(ref.shape[2:], ref.dtype)
    for group, keep, got in zip(groups, keeps, gots):

        def gather(index, carry, group=group, keep=keep, got=got):
            tile = tile_of(index, group, tiles)
            for part in range(2):
                mixed[part, pl.ds(core, views, stride=2), :] = keep[index, part]
                mixed[part, pl.ds(1 - core, views, stride=2), :] = got[index, part]
                high, low = split(mixed[part])
                high_all[part, tile + 1] = high
                low_all[part, tile + 1] = low
            return carry

        lax.fori_loop(0, 2 * group[1], gather, 0, unroll=2)

    batch = 4

    def produce(index, carry):
        first = index * batch

        def window(ref):
            pieces = []
            for part in range(2):
                begin = first if part == 0 else tiles - first - batch
                for section in range(3):
                    if part == 0:
                        piece = ref[0, pl.ds(begin + section, batch)]
                    else:
                        piece = jnp.stack(
                            [ref[1, begin + section + batch - 1 - i] for i in range(batch)]
                        )
                    pieces.append(piece.reshape(batch * 2 * views, LANES))
            return jnp.concatenate(pieces, axis=1)

        high, low = window(high_all), window(low_all)
        total = dot(high, high_ref[...]) + dot(low, high_ref[...]) + dot(high, low_ref[...])
        for i in range(batch):
            block = total[2 * views * i : 2 * views * (i + 1)].reshape(views, 2, 2 * LANES)
            at = pl.multiple_of((first + i) * 2 * LANES, 2 * LANES)
            out_ref[:, :, pl.ds(at, 2 * LANES)] = block
        return carry

    lax.fori_loop(0, tiles // batch, produce, 0)


def ramp_filter(groups, tiles, keeps, gots):
    views = keeps[0].shape[2]
    high, low = filter_matrix()
    stored = pltpu.VMEM((2, tiles + 2, 2 * views, LANES), jnp.bfloat16)
    return call(
        functools.partial(filter_body, groups, tiles),
        [f32(views, 2, 2 * tiles * LANES)],
        [pltpu.VMEM((2, 2 * views, LANES), jnp.float32), stored, stored],
        (high, low, *keeps, *gots),
        6 * tiles * 2 * views * 2 * WINDOW * 2 * LANES,
        5 << 20,
    )[0]


def permuted(value, axis, target):
    count = lax.axis_size(axis)
    pairs = [(i, target(i)) for i in range(count)]
    return lax.ppermute(value, axis, [(i, j) for i, j in pairs if 0 <= j < count])


def exchanged_blocks(group, tiles, view_offset, conj_offset, own):
    devices = lax.axis_size("ang")
    half = group[1]
    if devices == 8:
        by_y = permuted(own[:half], "ang", lambda i: i ^ 4)
        by_x = permuted(own[half:], "ang", lambda i: i ^ 2)
        for_x, for_y = select_views(group, tiles, view_offset, conj_offset, own, by_y, by_x)
        from_x = permuted(for_x, "ang", lambda i: i ^ 2)
        from_y = permuted(for_y, "ang", lambda i: i ^ 4)
        return [own, by_y, by_x, from_x, from_y]

    def ahead(part, chips):
        return permuted(part, "ang", lambda i: (i - 2 * chips) % devices)

    turned = devices // 4
    return [
        own,
        ahead(own[:, 32:], -1),
        ahead(own[:, :32], 1),
        ahead(own[:, 16:], turned - 1),
        ahead(own, turned),
        ahead(own[:, :48], turned + 1),
    ]


def on_device(
    sinogram, col_weights, col_start, view_offset, row_offset, conj_offset, ang_weights, row_weights
):
    tiles = col_weights.shape[0]
    views = sinogram.shape[0]
    exchanged = lax.axis_size("ang") == 8
    core = lax.axis_index("ang") % 2
    groups = ((0, tiles // 4), (tiles // 4, tiles // 4))
    keeps, gots = [], []
    halos = []
    for group in groups:
        own = resample(group, col_start, sinogram, col_weights)
        prev = permuted(own, "row", lambda i: i + 1)
        after = permuted(own, "row", lambda i: i - 1)
        halos.append((prev, own, after))
    blocks = []
    for number, group in enumerate(groups):
        prev, own, after = halos[number]
        if number:
            prev, after, blocks[-1] = lax.optimization_barrier((prev, after, blocks[-1]))
        keep, send = interpolate_rows(group, tiles, row_offset, prev, own, after, row_weights)
        got = permuted(send, "ang", lambda i: i ^ 1)
        blocks.append(lax.dynamic_update_slice(keep, got, (0, (1 - core) * views, 0)))
    for group, block in zip(groups, blocks):
        parts = exchanged_blocks(group, tiles, view_offset, conj_offset, block)
        keep, send = interpolate_views(
            group, tiles, exchanged, view_offset, conj_offset, ang_weights, parts
        )
        keeps.append(keep)
        gots.append(permuted(send, "ang", lambda i: i ^ 1))
    return ramp_filter(groups, tiles, keeps, gots)


def solution(mesh):
    return jax.shard_map(
        on_device,
        mesh=mesh,
        in_specs=(P("ang", "row", None), P(), P(), P(), P(), P(), P(), P()),
        out_specs=P("ang", "row", None),
        check_vma=False,
    )
```

```python
import functools
import math

import jax
import jax.numpy as jnp
import numpy as np
from jax import lax
from jax.experimental import pallas as pl
from jax.experimental.pallas import tpu as pltpu
from jax.sharding import PartitionSpec as P

KR = 256
GROUPS = ((0, 8), (8, 8))
LANES = 128
WINDOW = 3 * LANES
VMEM = pl.BlockSpec(memory_space=pltpu.VMEM)
SMEM = pl.BlockSpec(memory_space=pltpu.SMEM)
ANY = pl.BlockSpec(memory_space=pl.ANY)
PARAMS = pltpu.CompilerParams(vmem_limit_bytes=48 * 1024 * 1024)


COST = pl.CostEstimate(flops=1, bytes_accessed=1, transcendentals=0)
ROWS_COST = pl.CostEstimate(flops=1 << 32, bytes_accessed=1 << 26, transcendentals=0)


def call(body, outs, scratch, args, cost=COST):
    smem = [a.dtype == jnp.int32 for a in args]
    return pl.pallas_call(
        body,
        out_shape=outs,
        in_specs=[SMEM if s else VMEM for s in smem],
        out_specs=[VMEM] * len(outs),
        scratch_shapes=scratch,
        compiler_params=PARAMS,
        cost_estimate=cost,
    )(*args)


def f32(*shape):
    return jax.ShapeDtypeStruct(shape, jnp.float32)


def tile_of(index, group, tiles):
    first, half = group
    return jnp.where(index < half, first + index, tiles - first - 2 * half + index)


def split(x):
    high = x.astype(jnp.bfloat16)
    low = (x - high.astype(jnp.float32)).astype(jnp.bfloat16)
    return high, low


def dot(a, b):
    return jnp.dot(a, b, preferred_element_type=jnp.float32)


def resample_body(group, start_any, sino_any, weights_any, out_ref, start_ref, sino_ref, weights_ref, sems):
    tiles, band, _ = weights_any.shape
    views, rows, cols = sino_any.shape
    first, half = group
    quarter = views // 4
    copies = [pltpu.make_async_copy(start_any, start_ref, sems.at[0])]
    for i in range(4):
        part = pl.ds(quarter * i, quarter)
        copies.append(pltpu.make_async_copy(sino_any.at[part], sino_ref.at[part], sems.at[1 + i]))
    for i, begin in enumerate((first, tiles - first - half)):
        source = weights_any.at[pl.ds(begin, half)]
        copies.append(pltpu.make_async_copy(source, weights_ref.at[pl.ds(half * i, half)], sems.at[5 + i]))
    for copy in copies:
        copy.start()
    for copy in copies:
        copy.wait()

    def step(index, carry):
        start = start_ref[tile_of(index, group, tiles)]
        base = jnp.minimum(start // LANES * LANES, cols - WINDOW)
        shift = start - base
        slab = sino_ref[:, :, pl.ds(pl.multiple_of(base, LANES), WINDOW)]
        slab = slab.reshape(views * rows, WINDOW)
        slab = pltpu.roll(slab, WINDOW - shift, 1)[:, :band]
        high, low = split(slab)
        weights = weights_ref[index]
        out_ref[index] = dot(high, weights) + dot(low, weights)
        return carry

    lax.fori_loop(0, 2 * half, step, 0, unroll=2)


def resample(group, start, sino, weights):
    views, rows, cols = sino.shape
    count = 2 * group[1]
    return pl.pallas_call(
        functools.partial(resample_body, group),
        out_shape=f32(count, views * rows, LANES),
        in_specs=[ANY] * 3,
        out_specs=VMEM,
        scratch_shapes=[
            pltpu.SMEM(start.shape, jnp.int32),
            pltpu.VMEM(sino.shape, jnp.float32),
            pltpu.VMEM((count, *weights.shape[1:]), weights.dtype),
            pltpu.SemaphoreType.DMA((7,)),
        ],
        compiler_params=pltpu.CompilerParams(vmem_limit_bytes=(60 if group[0] == 0 else 40) << 20),
        cost_estimate=COST,
    )(start, sino, weights)


def rows_body(group, tiles, offset_ref, prev_ref, own_ref, next_ref, weights_ref, keep_ref, send_ref, stack):
    count, height, _ = own_ref.shape
    views = height // 2
    core = lax.axis_index("ang") % 2

    def step(index, slot):
        tile = tile_of(index, group, tiles)
        offset = offset_ref[tile]
        stack[slot, 0:height] = prev_ref[index]
        stack[slot, height : 2 * height] = own_ref[index]
        stack[slot, 2 * height : 3 * height] = next_ref[index]
        weights = weights_ref[:, pl.ds(pl.multiple_of(tile * LANES, LANES), LANES)]

        def picked(row):
            lifted = row + 2
            first = lifted // 2 * height + lifted % 2
            return stack[slot, pl.ds(first, views, stride=2), :]

        for out_ref, row in ((keep_ref, core), (send_ref, 1 - core)):
            lower = picked(row + offset)
            upper = picked(row + offset + 1)
            mixed = weights[0:1] * lower + weights[1:2] * upper
            out_ref[index] = mixed

    def pair(index, carry):
        step(2 * index, 0)
        step(2 * index + 1, 1)
        return carry

    lax.fori_loop(0, count // 2, pair, 0)


def interpolate_rows(group, tiles, offset, prev, own, after, weights):
    count, height, _ = own.shape
    return call(
        functools.partial(rows_body, group, tiles),
        [f32(count, height // 2, LANES)] * 2,
        [pltpu.VMEM((2, 3 * height, LANES), jnp.float32)],
        (offset, prev, own, after, weights),
        ROWS_COST,
    )


def merge_body(keep_ref, got_ref, *out_refs):
    half, views, _ = keep_ref.shape
    half //= 2
    core = lax.axis_index("ang") % 2
    mine = pl.multiple_of(core * views, 8)
    other = pl.multiple_of((1 - core) * views, 8)
    for part, out_ref in enumerate(out_refs):

        def step(index, slot, part=part, out_ref=out_ref):
            out_ref[index, pl.ds(mine, views)] = keep_ref[part * half + index]
            out_ref[index, pl.ds(other, views)] = got_ref[part * half + index]

        paired(step, half)


def merge(keep, got):
    count, views, _ = keep.shape
    return call(merge_body, [f32(count // 2, 2 * views, LANES)] * 2, [], (keep, got))


def select_body(
    group, tiles, view_ref, conj_ref, low_ref, high_ref, by_y_ref, by_x_ref, for_x_ref, for_y_ref, stack
):
    half = group[1]
    _, chip_views, lanes = low_ref.shape
    side = lax.axis_index("ang") // 2 % 2

    def shifts(index):
        tile = tile_of(index, group, tiles)
        shift = view_ref[tile]
        return shift, shift + conj_ref[tiles - 1 - tile]

    def slots(low, high):
        return low + lax.broadcasted_iota(jnp.int32, (high - low, lanes), 0)

    def across_x(index, slot):
        shift, opposite = shifts(index)
        own_at = pl.multiple_of((1 - side) * chip_views, 8)
        got_at = pl.multiple_of(side * chip_views, 8)
        stack[slot, pl.ds(own_at, chip_views)] = low_ref[index]
        stack[slot, pl.ds(got_at, chip_views)] = by_y_ref[index]
        near, far = stack.at[slot, 0:64], stack.at[slot, 64:128]
        for_x_ref[index, 0:32] = jnp.where(slots(0, 32) >= shift + 32, far[32:64], near[0:32])
        for_x_ref[index, 32:80] = jnp.where(slots(0, 48) >= opposite + 48, near[16:64], far[0:48])

    def across_y_first(index, slot):
        shift, opposite = shifts(half + index)
        stack[slot, 0:64] = high_ref[index]
        stack[slot, 64:128] = by_x_ref[index]
        both = stack.at[slot]
        for_y_ref[index, 0:40] = jnp.where(slots(0, 40) >= opposite, both[0:40], both[72:112])
        for_y_ref[index, 40:56] = both[40:56]
        for_y_ref[index, 56:72] = jnp.where(slots(56, 72) >= 88 + shift, both[96:112], both[56:72])
        for_y_ref[index, 72:88] = both[112:128]

    def across_y_last(index, slot):
        shift, opposite = shifts(half + index)
        stack[slot, 0:64] = by_x_ref[index]
        stack[slot, 64:128] = high_ref[index]
        both = stack.at[slot]
        for_y_ref[index, 0:16] = both[0:16]
        for_y_ref[index, 16:32] = jnp.where(slots(16, 32) < shift + 3, both[16:32], both[56:72])
        for_y_ref[index, 32:48] = both[72:88]
        for_y_ref[index, 48:88] = jnp.where(slots(48, 88) < 91 + opposite, both[88:128], both[16:56])

    paired(across_x, half)
    pl.when(side == 0)(lambda: paired(across_y_first, half))
    pl.when(side == 1)(lambda: paired(across_y_last, half))


def paired(step, count):
    def pair(index, carry):
        step(2 * index, 0)
        step(2 * index + 1, 1)
        return carry

    lax.fori_loop(0, count // 2, pair, 0)


def select_views(group, tiles, view_offset, conj_offset, low, high, by_y, by_x):
    half = group[1]
    return call(
        functools.partial(select_body, group, tiles),
        [f32(half, 80, LANES), f32(half, 88, LANES)],
        [pltpu.VMEM((2, 128, LANES), jnp.float32)],
        (view_offset, conj_offset, low, high, by_y, by_x),
    )


def views_body(group, tiles, exchanged, view_ref, conj_ref, weights_ref, *refs):
    *blocks, keep_ref, send_ref, stack = refs
    half = group[1]
    views = keep_ref.shape[2]
    index_ang = lax.axis_index("ang")
    side, core = index_ang // 2 % 2, index_ang % 2
    taps = weights_ref.shape[0]

    def interpolate(index, slot):
        tile = tile_of(index, group, tiles)
        weights = weights_ref[:, pl.ds(pl.multiple_of(tile * LANES, LANES), LANES)]
        shift = view_ref[tile]
        opposite = shift + conj_ref[tiles - 1 - tile]
        for part, by in ((0, 32 + shift), (1, 176 + opposite)):
            for out_ref, first in ((keep_ref, core), (send_ref, 1 - core)):
                begin = by + first * views
                total = weights[0:1] * stack[slot, pl.ds(begin, views)]
                for tap in range(1, taps):
                    total = total + weights[tap : tap + 1] * stack[slot, pl.ds(begin + tap, views)]
                out_ref[index, part] = total

    def filled(slot, *parts):
        at = 0
        for part in parts:
            stack[slot, at : at + part.shape[0]] = part[...]
            at += part.shape[0]

    if not exchanged:
        for part in range(2):

            def whole(index, slot, part=part):
                filled(slot, *(ref.at[index] for ref in blocks[part::2]))
                interpolate(part * half + index, slot)

            paired(whole, half)
        return
    own_low, own_high, by_y, by_x, from_x, from_y = blocks

    def first_half(index, slot):
        near, far = from_x.at[index, 0:32], from_x.at[index, 32:80]
        filled(slot, near, own_low.at[index], near, far, by_y.at[index], far)
        interpolate(index, slot)

    def last_half_first(index, slot):
        got = from_y.at[index]
        beside = by_x.at[index]
        filled(
            slot, got.at[56:88], own_high.at[index], beside.at[0:32], beside.at[16:64], got.at[0:72], got.at[0:40]
        )
        interpolate(half + index, slot)

    def last_half_last(index, slot):
        got = from_y.at[index]
        beside = by_x.at[index]
        filled(
            slot, beside.at[32:64], own_high.at[index], got.at[0:32], got.at[48:88], got.at[16:88], beside.at[0:48]
        )
        interpolate(half + index, slot)

    paired(first_half, half)
    pl.when(side == 0)(lambda: paired(last_half_first, half))
    pl.when(side == 1)(lambda: paired(last_half_last, half))


def interpolate_views(group, tiles, exchanged, view_offset, conj_offset, weights, blocks):
    count = 2 * group[1]
    views = blocks[0 if exchanged else 2].shape[1] // 2
    return call(
        functools.partial(views_body, group, tiles, exchanged),
        [f32(count, 2, views, LANES)] * 2,
        [pltpu.VMEM((2, 288, LANES), jnp.float32)],
        (view_offset, conj_offset, weights, *blocks),
    )


def ramp(lag):
    lag = lag.astype(np.float64)
    odd = np.abs(lag) % 2 == 1
    values = np.where(lag == 0, 0.25, np.where(odd, -1.0 / (math.pi**2 * np.maximum(lag * lag, 1.0)), 0.0))
    return np.where(np.abs(lag) <= KR, values, 0.0).astype(np.float32)


def filter_matrix():
    column = np.arange(WINDOW)[:, None]
    place = np.arange(2 * LANES)[None, :]
    lag = place - 2 * (column - LANES)
    even = ramp(lag)
    odd = ramp(lag - 1)[::-1]
    whole = np.concatenate([even, odd], axis=0)
    high = whole.astype(jnp.bfloat16)
    low = (whole - high.astype(np.float32)).astype(jnp.bfloat16)
    return jnp.asarray(high), jnp.asarray(low)


def stage_spans(groups, number, tiles):
    first, half = groups[number]
    begin = first - 1 if number else 0
    if number == len(groups) - 1:
        ranges = [(begin, tiles - begin)]
    else:
        ranges = [(begin, first + half - 1), (tiles - first - half + 1, tiles - begin)]
    spans = []
    for low, high in ranges:
        while low < high:
            count = min(4, high - low)
            spans.append((low, count))
            low += count
    return spans


def filter_body(groups, number, tiles, high_ref, low_ref, *refs):
    parts = refs[: 4 if number else 2]
    out_any, mixed, high_all, low_all, result, sems = refs[-6:]
    views = out_any.shape[0]
    core = lax.axis_index("ang") % 2
    if number == 0:
        for ref in (high_all, low_all):
            for part in range(2):
                ref[part, 0] = jnp.zeros(ref.shape[2:], ref.dtype)
                ref[part, tiles + 1] = jnp.zeros(ref.shape[2:], ref.dtype)

    def gather(group, keep, got, index, slot):
        tile = tile_of(index, group, tiles)
        for part in range(2):
            mixed[slot, part, pl.ds(core, views, stride=2), :] = keep[index, part]
            mixed[slot, part, pl.ds(1 - core, views, stride=2), :] = got[index, part]
            high, low = split(mixed[slot, part])
            high_all[part, tile + 1] = high
            low_all[part, tile + 1] = low

    paired(functools.partial(gather, groups[number], *parts[:2]), 2 * groups[number][1])
    if number:
        half = groups[number - 1][1]
        for index in range(half - 2, half + 2):
            gather(groups[number - 1], *parts[2:], index, index % 2)

    copies = []
    for place, (first, count) in enumerate(stage_spans(groups, number, tiles)):

        def window(ref):
            pieces = []
            for section in range(3):
                piece = ref[0, first + section : first + section + count]
                pieces.append(piece.reshape(count * 2 * views, LANES))
            for section in range(3):
                last = tiles - 1 - first + section
                piece = jnp.stack([ref[1, last - i] for i in range(count)])
                pieces.append(piece.reshape(count * 2 * views, LANES))
            return jnp.concatenate(pieces, axis=1)

        high, low = window(high_all), window(low_all)
        total = dot(high, high_ref[...]) + dot(low, high_ref[...]) + dot(high, low_ref[...])
        for i in range(count):
            block = total[2 * views * i : 2 * views * (i + 1)].reshape(views, 2, 2 * LANES)
            result[:, :, (first + i) * 2 * LANES : (first + i + 1) * 2 * LANES] = block
        columns = pl.ds(first * 2 * LANES, count * 2 * LANES)
        copy = pltpu.make_async_copy(
            result.at[:, :, columns], out_any.at[:, :, columns], sems.at[place]
        )
        copy.start()
        copies.append(copy)
    for copy in copies:
        copy.wait()


def ramp_filter(groups, number, tiles, keeps, gots, out):
    views = keeps[0].shape[2]
    args = [*filter_matrix(), keeps[number], gots[number]]
    if number:
        args += [keeps[number - 1], gots[number - 1], out]
    stored = pltpu.VMEM((2, tiles + 2, 2 * views, LANES), jnp.bfloat16)
    shape = f32(views, 2, 2 * tiles * LANES)
    return pl.pallas_call(
        functools.partial(filter_body, groups, number, tiles),
        out_shape=shape,
        in_specs=[VMEM] * 6 + [ANY] if number else [VMEM] * 4,
        out_specs=ANY,
        scratch_shapes=[
            pltpu.VMEM((2, 2, 2 * views, LANES), jnp.float32),
            stored,
            stored,
            pltpu.VMEM(shape.shape, jnp.float32),
            pltpu.SemaphoreType.DMA((len(stage_spans(groups, number, tiles)),)),
        ],
        input_output_aliases={6: 0} if number else {},
        compiler_params=PARAMS,
        cost_estimate=COST,
    )(*args)


def permuted(value, axis, target):
    count = lax.axis_size(axis)
    pairs = [(i, target(i)) for i in range(count)]
    return lax.ppermute(value, axis, [(i, j) for i, j in pairs if 0 <= j < count])


def first_exchange(low, high):
    if lax.axis_size("ang") == 8:
        by_y = permuted(low, "ang", lambda i: i ^ 4)
        by_x = permuted(high, "ang", lambda i: i ^ 2)
        return [by_y, by_x]
    return []


def second_exchange(group, tiles, view_offset, conj_offset, low, high, first):
    devices = lax.axis_size("ang")
    if first:
        for_x, for_y = select_views(group, tiles, view_offset, conj_offset, low, high, *first)
        from_x = permuted(for_x, "ang", lambda i: i ^ 2)
        from_y = permuted(for_y, "ang", lambda i: i ^ 4)
        return [low, high, *first, from_x, from_y]

    def ahead(begin, end, chips):
        def target(i):
            return (i - 2 * chips) % devices

        return [permuted(part[:, begin:end], "ang", target) for part in (low, high)]

    turned = devices // 4
    return [
        *ahead(32, 64, -1),
        low,
        high,
        *ahead(0, 32, 1),
        *ahead(16, 64, turned - 1),
        *ahead(0, 64, turned),
        *ahead(0, 48, turned + 1),
    ]


def on_device(
    sinogram, col_weights, col_start, view_offset, row_offset, conj_offset, ang_weights, row_weights
):
    tiles = col_weights.shape[0]
    exchanged = lax.axis_size("ang") == 8
    groups = GROUPS
    halos, owns = [], []
    for group in groups:
        own = resample(group, col_start, sinogram, col_weights)
        prev = permuted(own, "row", lambda i: i + 1)
        after = permuted(own, "row", lambda i: i - 1)
        halos.append((prev, own, after))
    for group, (prev, own, after) in zip(groups, halos):
        keep, send = interpolate_rows(group, tiles, row_offset, prev, own, after, row_weights)
        got = permuted(send, "ang", lambda i: i ^ 1)
        owns.append(merge(keep, got))
    keeps, gots = [], []
    out = None
    for number, group in enumerate(groups):
        low, high = owns[number]
        first = first_exchange(low, high)
        if keeps:
            first, keeps[-1] = lax.optimization_barrier((first, keeps[-1]))
        blocks = second_exchange(group, tiles, view_offset, conj_offset, low, high, first)
        if keeps:
            out = ramp_filter(groups, number - 1, tiles, keeps, gots, out)
            blocks[-1], out = lax.optimization_barrier((blocks[-1], out))
        keep, send = interpolate_views(
            group, tiles, exchanged, view_offset, conj_offset, ang_weights, blocks
        )
        keeps.append(keep)
        gots.append(permuted(send, "ang", lambda i: i ^ 1))
    return ramp_filter(groups, len(groups) - 1, tiles, keeps, gots, out)


def solution(mesh):
    return jax.shard_map(
        on_device,
        mesh=mesh,
        in_specs=(P("ang", "row", None), P(), P(), P(), P(), P(), P(), P()),
        out_specs=P("ang", "row", None),
        check_vma=False,
    )
```

```python
import functools
import math

import jax
import jax.numpy as jnp
import numpy as np
from jax import lax
from jax.experimental import pallas as pl
from jax.experimental.pallas import tpu as pltpu
from jax.sharding import PartitionSpec as P

KR = 256
OUTER, INNER = (0, 6), (6, 10)
LANES = 128
WINDOW = 3 * LANES
SLOTS = 88
VMEM = pl.BlockSpec(memory_space=pltpu.VMEM)
SMEM = pl.BlockSpec(memory_space=pltpu.SMEM)
ANY = pl.BlockSpec(memory_space=pl.ANY)
SHORT = pl.CostEstimate(flops=1, bytes_accessed=1, transcendentals=0)


def cycles(number):
    return pl.CostEstimate(flops=number << 19, bytes_accessed=1, transcendentals=0)


def call(body, outs, scratch, args, cost=SHORT, after=(), specs=None, limit=48, out=VMEM, aliases={}):
    if specs is None:
        specs = [SMEM if a.dtype == jnp.int32 else VMEM for a in args]
    taken = len(args)

    def kernel(*refs):
        body(*refs[:taken], *refs[taken + len(after) :])

    return pl.pallas_call(
        kernel,
        out_shape=outs,
        in_specs=[*specs, *[ANY] * len(after)],
        out_specs=[out] * len(outs),
        scratch_shapes=scratch,
        input_output_aliases=aliases,
        compiler_params=pltpu.CompilerParams(vmem_limit_bytes=limit << 20),
        cost_estimate=cost,
    )(*args, *after)


def f32(*shape):
    return jax.ShapeDtypeStruct(shape, jnp.float32)


def position():
    index = lax.axis_index("ang")
    return index // 2 % 2, index % 2


def tile_of(index, group, tiles, core):
    first, half = group
    return index + jnp.where(core == 0, first, tiles - first - half)


def split(x):
    high = x.astype(jnp.bfloat16)
    low = (x - high.astype(jnp.float32)).astype(jnp.bfloat16)
    return high, low


def dot(a, b):
    return jnp.dot(a, b, preferred_element_type=jnp.float32)


def paired(step, count):
    def pair(index, carry):
        step(2 * index, 0)
        step(2 * index + 1, 1)
        return carry

    lax.fori_loop(0, count // 2, pair, 0)
    if count % 2:
        step(count - 1, 0)


def resample_body(group, whole, apart, start_any, weights_any, *refs):
    number = 2 if whole else 1
    slabs_any, *rest = refs[:number], *refs[number:]
    done_ref = None if whole or len(rest) == 6 else rest.pop(0)
    out_ref, start_ref, weights_ref, sino_ref, sems, stack = rest
    tiles = weights_any.shape[0]
    band = weights_any.shape[1]
    views, rows, cols = slabs_any[0].shape
    height = views * rows
    _, core = position()
    mine = pl.multiple_of(core * height, 8)
    other = pl.multiple_of((1 - core) * height, 8)
    first = tile_of(0, group, tiles, core)
    copies = [
        pltpu.make_async_copy(start_any, start_ref, sems.at[0]),
        pltpu.make_async_copy(weights_any.at[pl.ds(first, group[1])], weights_ref, sems.at[1]),
    ]
    for i, slab_any in enumerate(slabs_any):
        copies.append(pltpu.make_async_copy(slab_any, sino_ref.at[i], sems.at[2 + i]))
    for copy in copies:
        copy.start()
    for copy in copies:
        copy.wait()

    def step(index, slot):
        start = start_ref[first + index]
        base = jnp.minimum(start // LANES * LANES, cols - WINDOW)
        shift = start - base
        columns = pl.ds(pl.multiple_of(base, LANES), WINDOW)
        slab = sino_ref[:, :, :, columns].reshape(number * height, WINDOW)
        slab = pltpu.roll(slab, WINDOW - shift, 1)[:, :band]
        high, low = split(slab)
        weights = weights_ref[index]
        total = dot(high, weights) + dot(low, weights)
        if whole:
            target = stack.at[slot] if apart else out_ref.at[index]
            target[pl.ds(mine, height)] = total[:height]
            target[pl.ds(other, height)] = total[height:]
            if apart:
                for row in range(rows):
                    out_ref[index, row] = stack[slot, pl.ds(row, 2 * views, stride=rows), :]
        elif done_ref is None:
            out_ref[index] = total
        else:
            out_ref[index, pl.ds(mine, height)] = done_ref[index]
            out_ref[index, pl.ds(other, height)] = total

    paired(step, group[1])


def resample(group, start, weights, slabs, done=(), apart=False, after=()):
    views, rows, _ = slabs[0].shape
    whole = len(slabs) == 2
    height = views * rows * (2 if whole or done else 1)
    return call(
        functools.partial(resample_body, group, whole, apart),
        [f32(group[1], rows, 2 * views, LANES) if apart else f32(group[1], height, LANES)],
        [
            pltpu.SMEM(start.shape, jnp.int32),
            pltpu.VMEM((group[1], *weights.shape[1:]), weights.dtype),
            pltpu.VMEM((len(slabs), *slabs[0].shape), jnp.float32),
            pltpu.SemaphoreType.DMA((4,)),
            pltpu.VMEM((2, 2 * views * rows + 8, LANES), jnp.float32),
        ],
        (start, weights, *slabs, *done),
        cost=cycles(4000) if apart else SHORT,
        after=after,
        specs=[ANY] * (2 + len(slabs)) + [VMEM] * len(done),
        limit=48 if whole or done else 60,
    )[0]


def rows_body(group, tiles, offset_ref, even_ref, odd_ref, own_ref, weights_ref, out_ref, stack):
    count, height, _ = own_ref.shape
    views = height // 2
    _, core = position()
    after = lax.axis_index("row") % 2 == 0
    even_at = pl.multiple_of(jnp.where(after, 2 * height, 0), 8)
    odd_at = pl.multiple_of(jnp.where(after, 0, 2 * height), 8)

    def step(index, slot):
        tile = tile_of(index, group, tiles, core)
        offset = offset_ref[tile]
        stack[slot, pl.ds(even_at, height)] = even_ref[index]
        stack[slot, pl.ds(odd_at, height)] = odd_ref[index]
        stack[slot, height : 2 * height] = own_ref[index]
        weights = weights_ref[:, pl.ds(pl.multiple_of(tile * LANES, LANES), LANES)]

        def picked(row):
            lifted = row + 2
            first = lifted // 2 * height + lifted % 2
            return stack[slot, pl.ds(first, views, stride=2), :]

        terms = [picked(row + offset) for row in range(3)]
        for row in range(2):
            out_ref[index, row] = weights[0:1] * terms[row] + weights[1:2] * terms[row + 1]

    paired(step, count)


def interpolate_rows(group, tiles, offset, even, odd, own, weights, after):
    count, height, _ = own.shape
    return call(
        functools.partial(rows_body, group, tiles),
        [f32(count, 2, height // 2, LANES)],
        [pltpu.VMEM((2, 3 * height + 8, LANES), jnp.float32)],
        (offset, even, odd, own, weights),
        after=after,
    )[0]


def last_rows_body(group, tiles, offset_ref, even_ref, odd_ref, own_ref, weights_ref, keep_ref, send_ref, stack):
    count, parts, rows, chip_views, _ = own_ref.shape
    views = chip_views // 2
    _, core = position()
    after = lax.axis_index("row") % 2 == 0
    even_at = jnp.where(after, 2 * rows, 0)
    odd_at = jnp.where(after, 0, 2 * rows)
    mine = pl.multiple_of(core * views, 8)
    other = pl.multiple_of((1 - core) * views, 8)

    def step(index, slot):
        tile = tile_of(index, group, tiles, core)
        first = offset_ref[tile] + rows
        weights = weights_ref[:, pl.ds(pl.multiple_of(tile * LANES, LANES), LANES)]
        for part in range(parts):
            for row in range(rows):
                stack[slot, even_at + row] = even_ref[index, part, row]
                stack[slot, odd_at + row] = odd_ref[index, part, row]
                stack[slot, rows + row] = own_ref[index, part, row]
            for out_ref, begin in ((keep_ref, mine), (send_ref, other)):
                terms = [stack[slot, first + i, pl.ds(begin, views)] for i in range(rows + 1)]
                for row in range(rows):
                    out_ref[index, part, row] = weights[0:1] * terms[row] + weights[1:2] * terms[row + 1]

    paired(step, count)


def interpolate_rows_last(group, tiles, offset, even, odd, own, weights):
    count, parts, rows, chip_views, _ = own.shape
    return call(
        functools.partial(last_rows_body, group, tiles),
        [f32(count, parts, rows, chip_views // 2, LANES)] * 2,
        [pltpu.VMEM((2, 3 * rows, chip_views, LANES), jnp.float32)],
        (offset, even, odd, own, weights),
        cycles(4000),
    )


def select_body(group, tiles, view_ref, conj_ref, own_ref, got_ref, out_ref, stack):
    count, rows, chip_views, lanes = own_ref.shape
    side, core = position()

    def shifts(index):
        tile = tile_of(index, group, tiles, core)
        shift = view_ref[tile]
        return shift, shift + conj_ref[tiles - 1 - tile]

    def slots(low, high):
        return low + lax.broadcasted_iota(jnp.int32, (high - low, lanes), 0)

    def across_x(index, slot):
        shift, opposite = shifts(index)
        own_at = pl.multiple_of((1 - side) * chip_views, 8)
        got_at = pl.multiple_of(side * chip_views, 8)
        for row in range(rows):
            out = out_ref.at[index, row]
            both = stack.at[slot, row]
            both[pl.ds(own_at, chip_views)] = own_ref[index, row]
            both[pl.ds(got_at, chip_views)] = got_ref[index, row]
            out[0:32] = jnp.where(slots(0, 32) >= shift + 32, both[96:128], both[0:32])
            out[32:80] = jnp.where(slots(0, 48) >= opposite + 48, both[16:64], both[64:112])
            out[80:88] = jnp.zeros((8, lanes), jnp.float32)

    def across_y_first(index, slot):
        shift, opposite = shifts(index)
        for row in range(rows):
            out = out_ref.at[index, row]
            both = stack.at[slot, row]
            both[0:64] = own_ref[index, row]
            both[64:128] = got_ref[index, row]
            out[0:40] = jnp.where(slots(0, 40) >= opposite, both[0:40], both[72:112])
            out[40:56] = both[40:56]
            out[56:72] = jnp.where(slots(56, 72) >= 88 + shift, both[96:112], both[56:72])
            out[72:88] = both[112:128]

    def across_y_last(index, slot):
        shift, opposite = shifts(index)
        for row in range(rows):
            out = out_ref.at[index, row]
            both = stack.at[slot, row]
            both[0:64] = got_ref[index, row]
            both[64:128] = own_ref[index, row]
            out[0:16] = both[0:16]
            out[16:32] = jnp.where(slots(16, 32) < shift + 3, both[16:32], both[56:72])
            out[32:48] = both[72:88]
            out[48:88] = jnp.where(slots(48, 88) < 91 + opposite, both[88:128], both[16:56])

    pl.when(core == 0)(lambda: paired(across_x, count))
    pl.when((core == 1) & (side == 0))(lambda: paired(across_y_first, count))
    pl.when((core == 1) & (side == 1))(lambda: paired(across_y_last, count))


def select_views(group, tiles, view_offset, conj_offset, own, got, after=()):
    count, rows, chip_views, _ = own.shape
    return call(
        functools.partial(select_body, group, tiles),
        [f32(count, rows, SLOTS, LANES)],
        [pltpu.VMEM((2, rows, 2 * chip_views, LANES), jnp.float32)],
        (view_offset, conj_offset, own, got),
        after=after,
    )[0]


def views_body(group, tiles, exchanged, view_ref, conj_ref, weights_ref, *refs):
    *blocks, stack = refs
    outs = blocks[3 if exchanged else 6 :]
    blocks = blocks[: 3 if exchanged else 6]
    count, _, rows, views, _ = outs[0].shape
    side, core = position()
    firsts = (core, 1 - core) if len(outs) == 2 else (0,)
    taps = weights_ref.shape[0]

    def interpolate(index, slot, row):
        tile = tile_of(index, group, tiles, core)
        weights = weights_ref[:, pl.ds(pl.multiple_of(tile * LANES, LANES), LANES)]
        shift = view_ref[tile]
        opposite = shift + conj_ref[tiles - 1 - tile]
        for part, by in ((0, 32 + shift), (1, 176 + opposite)):
            for out_ref, first in zip(outs, firsts):
                begin = by + first * views
                total = weights[0:1] * stack[slot, row, pl.ds(begin, views)]
                for tap in range(1, taps):
                    total = total + weights[tap : tap + 1] * stack[slot, row, pl.ds(begin + tap, views)]
                out_ref[index, part, row] = total

    def run(parts):
        def step(index, slot):
            for row in range(rows):
                at = 0
                for part in parts(*(ref.at[index, row] for ref in blocks)):
                    stack[slot, row, at : at + part.shape[0]] = part[...]
                    at += part.shape[0]
                interpolate(index, slot, row)

        paired(step, count)

    def from_neighbours(before, own, after, early, middle, late):
        return before, own, after, early, middle, late

    def from_x(own, beyond, got):
        near, far = got.at[0:32], got.at[32:80]
        return near, own, near, far, beyond, far

    def from_y_first(own, beside, got):
        return got.at[56:88], own, beside.at[0:32], beside.at[16:64], got.at[0:72], got.at[0:40]

    def from_y_last(own, beside, got):
        return beside.at[32:64], own, got.at[0:32], got.at[48:88], got.at[16:88], beside.at[0:48]

    if exchanged:
        pl.when(core == 0)(lambda: run(from_x))
        pl.when((core == 1) & (side == 0))(lambda: run(from_y_first))
        pl.when((core == 1) & (side == 1))(lambda: run(from_y_last))
    else:
        run(from_neighbours)


def interpolate_views(group, tiles, exchanged, view_offset, conj_offset, weights, blocks, pieces, cost=SHORT, after=()):
    count, rows, chip_views, _ = blocks[0 if exchanged else 1].shape
    return call(
        functools.partial(views_body, group, tiles, exchanged),
        [f32(count, 2, rows, chip_views // pieces, LANES)] * pieces,
        [pltpu.VMEM((2, rows, 288, LANES), jnp.float32)],
        (view_offset, conj_offset, weights, *blocks),
        cost,
        after,
    )


def ramp(lag):
    lag = lag.astype(np.float64)
    odd = np.abs(lag) % 2 == 1
    values = np.where(lag == 0, 0.25, np.where(odd, -1.0 / (math.pi**2 * np.maximum(lag * lag, 1.0)), 0.0))
    return np.where(np.abs(lag) <= KR, values, 0.0).astype(np.float32)


def filter_matrix():
    column = np.arange(WINDOW)[:, None]
    place = np.arange(2 * LANES)[None, :]
    lag = place - 2 * (column - LANES)
    whole = np.concatenate([ramp(lag), ramp(lag - 1)[::-1]], axis=0)
    high = whole.astype(jnp.bfloat16)
    low = (whole - high.astype(np.float32)).astype(jnp.bfloat16)
    return jnp.asarray(high), jnp.asarray(low)


def stage_spans(groups, number, tiles):
    first, half = groups[number]
    begin = first - 1 if number else 0
    if number == len(groups) - 1:
        ranges = [(begin, tiles - begin)]
    else:
        ranges = [(begin, first + half - 1), (tiles - first - half + 1, tiles - begin)]
    spans = []
    for low, high in ranges:
        while low < high:
            count = min(4, high - low)
            spans.append((low, count))
            low += count
    return spans


def filter_body(groups, number, tiles, high_ref, low_ref, *refs):
    parts = refs[: 4 if number else 2]
    out_any, mixed, high_all, low_all, result, sems = refs[-6:]
    views = out_any.shape[0]
    _, core = position()
    if number == 0:
        for ref in (high_all, low_all):
            for part in range(2):
                ref[part, 0] = jnp.zeros(ref.shape[2:], ref.dtype)
                ref[part, tiles + 1] = jnp.zeros(ref.shape[2:], ref.dtype)

    def gather(group, ref, owner, index, slot):
        tile = tile_of(index, group, tiles, owner)
        for part in range(2):
            for row in range(2):
                mixed[slot, part, pl.ds(row, views, stride=2), :] = ref[index, part, row]
            high, low = split(mixed[slot, part, 0 : 2 * views])
            high_all[part, tile + 1] = high
            low_all[part, tile + 1] = low

    for ref, owner in zip(parts[:2], (core, 1 - core)):
        paired(functools.partial(gather, groups[number], ref, owner), groups[number][1])
    if number:
        half = groups[number - 1][1]
        for ref, owner in zip(parts[2:], (core, 1 - core)):
            begin = jnp.where(owner == 0, half - 2, 0)
            for i in range(2):
                gather(groups[number - 1], ref, owner, begin + i, i)

    copies = []
    for place, (first, count) in enumerate(stage_spans(groups, number, tiles)):

        def window(ref):
            pieces = []
            for section in range(3):
                piece = ref[0, first + section : first + section + count]
                pieces.append(piece.reshape(count * 2 * views, LANES))
            for section in range(3):
                last = tiles - 1 - first + section
                piece = jnp.stack([ref[1, last - i] for i in range(count)])
                pieces.append(piece.reshape(count * 2 * views, LANES))
            return jnp.concatenate(pieces, axis=1)

        high, low = window(high_all), window(low_all)
        total = dot(high, high_ref[...]) + dot(low, high_ref[...]) + dot(high, low_ref[...])
        for i in range(count):
            block = total[2 * views * i : 2 * views * (i + 1)].reshape(views, 2, 2 * LANES)
            result[:, :, (first + i) * 2 * LANES : (first + i + 1) * 2 * LANES] = block
        columns = pl.ds(first * 2 * LANES, count * 2 * LANES)
        copy = pltpu.make_async_copy(
            result.at[:, :, columns], out_any.at[:, :, columns], sems.at[place]
        )
        copy.start()
        copies.append(copy)
    for copy in copies:
        copy.wait()


def ramp_filter(groups, number, tiles, keeps, gots, out):
    views = keeps[0].shape[3]
    args = [*filter_matrix(), keeps[number], gots[number]]
    if number:
        args += [keeps[number - 1], gots[number - 1], out]
    stored = pltpu.VMEM((2, tiles + 2, 2 * views, LANES), jnp.bfloat16)
    shape = f32(views, 2, 2 * tiles * LANES)
    return call(
        functools.partial(filter_body, groups, number, tiles),
        [shape],
        [
            pltpu.VMEM((2, 2, 2 * views + 8, LANES), jnp.float32),
            stored,
            stored,
            pltpu.VMEM(shape.shape, jnp.float32),
            pltpu.SemaphoreType.DMA((len(stage_spans(groups, number, tiles)),)),
        ],
        args,
        specs=[VMEM] * 6 + [ANY] if number else [VMEM] * 4,
        out=ANY,
        aliases={6: 0} if number else {},
        cost=SHORT if number else cycles(6000),
    )[0]


def permuted(value, axis, target):
    count = lax.axis_size(axis)
    pairs = [(i, target(i)) for i in range(count)]
    return lax.ppermute(value, axis, [(i, j) for i, j in pairs if 0 <= j < count])


def swapped(value):
    return permuted(value, "ang", lambda i: i ^ 1)


def row_pairs(own):
    even = permuted(own, "row", lambda i: i ^ 1)
    odd = permuted(own, "row", lambda i: ((i + 1) ^ 1) - 1)
    return even, odd


def first_exchange(own):
    if lax.axis_size("ang") == 8:
        return [permuted(own, "ang", lambda i: i ^ (2 if i % 2 else 4))]
    return []


def second_exchange(own, first, chosen):
    devices = lax.axis_size("ang")
    if first:
        return [own, *first, permuted(chosen[0], "ang", lambda i: i ^ (4 if i % 2 else 2))]

    def ahead(begin, end, chips):
        return permuted(own[:, :, begin:end], "ang", lambda i: (i - 2 * chips) % devices)

    turned = devices // 4
    return [
        ahead(32, 64, -1),
        own,
        ahead(0, 32, 1),
        ahead(16, 64, turned - 1),
        ahead(0, 64, turned),
        ahead(0, 48, turned + 1),
    ]


def on_device(
    sinogram, col_weights, col_start, view_offset, row_offset, conj_offset, ang_weights, row_weights
):
    tiles = col_weights.shape[0]
    exchanged = lax.axis_size("ang") == 8
    offsets = (view_offset, conj_offset)
    groups = (OUTER, INNER)

    beside = swapped(sinogram)
    inner = resample(INNER, col_start, col_weights, (sinogram,))
    inner = resample(INNER, col_start, col_weights, (beside,), (inner,))
    inner_halo = row_pairs(inner)
    outer = resample(
        OUTER, col_start, col_weights, (sinogram, beside), apart=True, after=(inner,)
    )

    first = first_exchange(outer)
    chosen = [select_views(OUTER, tiles, *offsets, outer, got) for got in first]
    parts = second_exchange(outer, first, chosen)
    (outer,) = interpolate_views(
        OUTER, tiles, exchanged, *offsets, ang_weights, parts, 1, cycles(5000)
    )
    outer_halo = row_pairs(outer)

    inner = interpolate_rows(INNER, tiles, row_offset, *inner_halo, inner, row_weights, chosen)
    first = first_exchange(inner)
    chosen = [select_views(INNER, tiles, *offsets, inner, got, (outer,)) for got in first]
    parts = second_exchange(inner, first, chosen)

    outer_keep, send = interpolate_rows_last(
        OUTER, tiles, row_offset, *outer_halo, outer, row_weights
    )
    outer_got = swapped(send)
    out = ramp_filter(groups, 0, tiles, [outer_keep], [outer_got], None)
    inner_keep, send = interpolate_views(
        INNER, tiles, exchanged, *offsets, ang_weights, parts, 2
    )
    inner_got = swapped(send)
    return ramp_filter(
        groups, 1, tiles, (outer_keep, inner_keep), (outer_got, inner_got), out
    )


def solution(mesh):
    return jax.shard_map(
        on_device,
        mesh=mesh,
        in_specs=(P("ang", "row", None), P(), P(), P(), P(), P(), P(), P()),
        out_specs=P("ang", "row", None),
        check_vma=False,
    )
```

```python
import functools
import math

import jax
import jax.numpy as jnp
import numpy as np
from jax import lax
from jax.experimental import pallas as pl
from jax.experimental.pallas import tpu as pltpu
from jax.sharding import PartitionSpec as P

KR = 256
OUTER, INNER = (0, 6), (6, 10)
LANES = 128
WINDOW = 3 * LANES
SLOTS = 88
VMEM = pl.BlockSpec(memory_space=pltpu.VMEM)
SMEM = pl.BlockSpec(memory_space=pltpu.SMEM)
ANY = pl.BlockSpec(memory_space=pl.ANY)
SHORT = pl.CostEstimate(flops=1, bytes_accessed=1, transcendentals=0)


def cycles(number):
    return pl.CostEstimate(flops=number << 19, bytes_accessed=1, transcendentals=0)


def call(body, outs, scratch, args, cost=SHORT, after=(), specs=None, limit=48, out=VMEM, aliases={}):
    if specs is None:
        specs = [SMEM if a.dtype == jnp.int32 else VMEM for a in args]
    taken = len(args)

    def kernel(*refs):
        body(*refs[:taken], *refs[taken + len(after) :])

    return pl.pallas_call(
        kernel,
        out_shape=outs,
        in_specs=[*specs, *[ANY] * len(after)],
        out_specs=[out] * len(outs),
        scratch_shapes=scratch,
        input_output_aliases=aliases,
        compiler_params=pltpu.CompilerParams(vmem_limit_bytes=limit << 20),
        cost_estimate=cost,
    )(*args, *after)


def hbm(x):
    return pltpu.with_memory_space_constraint(x, pltpu.HBM)


def f32(*shape):
    return jax.ShapeDtypeStruct(shape, jnp.float32)


def position():
    index = lax.axis_index("ang")
    return index // 2 % 2, index % 2


def tile_of(index, group, tiles, core):
    first, half = group
    return index + jnp.where(core == 0, first, tiles - first - half)


def split(x):
    high = x.astype(jnp.bfloat16)
    low = (x - high.astype(jnp.float32)).astype(jnp.bfloat16)
    return high, low


def dot(a, b):
    return jnp.dot(a, b, preferred_element_type=jnp.float32)


def dot_terms(high, low, b):
    both = dot(jnp.concatenate([high, low], axis=0), b)
    return both[: high.shape[0]] + both[high.shape[0] :]


def unrolled(step, count):
    for index in range(count):
        step(index, index % 2)


def paired(step, count):
    def pair(index, carry):
        step(2 * index, 0)
        step(2 * index + 1, 1)
        return carry

    lax.fori_loop(0, count // 2, pair, 0)
    if count % 2:
        step(count - 1, 0)


def resampled_tile(slab_refs, start, weights):
    cols = slab_refs[0].shape[2]
    base = jnp.minimum(start // LANES * LANES, cols - WINDOW)
    columns = pl.ds(pl.multiple_of(base, LANES), WINDOW)
    slabs = [ref[:, :, columns].reshape(-1, WINDOW) for ref in slab_refs]
    slab = jnp.concatenate(slabs, axis=0)
    slab = pltpu.roll(slab, WINDOW - (start - base), 1)[:, : weights.shape[0]]
    return dot_terms(*split(slab), weights)


def resample_own_body(group, start_any, weights_any, sino_any, out_ref, weights_ref, sino_ref, start_ref, sems):
    tiles = weights_any.shape[0]
    held = weights_ref.shape[0]
    first, half = group
    _, core = position()
    place = jnp.where(core == 0, first, held - first - half)
    origin = core * (tiles - held)
    later = jnp.where(core == 0, 0, half)
    needed = [
        pltpu.make_async_copy(start_any, start_ref, sems.at[0]),
        pltpu.make_async_copy(sino_any, sino_ref, sems.at[1]),
        pltpu.make_async_copy(
            weights_any.at[pl.ds(origin + place, half)], weights_ref.at[pl.ds(place, half)], sems.at[2]
        ),
    ]
    rest = pltpu.make_async_copy(
        weights_any.at[pl.ds(origin + later, held - half)],
        weights_ref.at[pl.ds(later, held - half)],
        sems.at[3],
    )
    for copy in (*needed, rest):
        copy.start()
    for copy in needed:
        copy.wait()

    def step(index, slot):
        start = start_ref[origin + place + index]
        out_ref[index] = resampled_tile([sino_ref], start, weights_ref[place + index])

    unrolled(step, half)
    rest.wait()


def resample_own(group, start, weights, sino):
    views, rows, _ = sino.shape
    held = weights.shape[0] // 2
    return call(
        functools.partial(resample_own_body, group),
        [
            f32(group[1], views * rows, LANES),
            jax.ShapeDtypeStruct((held, *weights.shape[1:]), weights.dtype),
            f32(*sino.shape),
        ],
        [pltpu.SMEM(start.shape, jnp.int32), pltpu.SemaphoreType.DMA((4,))],
        [hbm(x) for x in (start, weights, sino)],
        specs=[ANY] * 3,
    )


def resample_rest_body(group, tiles, start_ref, weights_ref, got_ref, done_ref, out_ref):
    held, (first, half) = weights_ref.shape[0], group
    height = done_ref.shape[1]
    _, core = position()
    place = jnp.where(core == 0, first, held - first - half)
    origin = core * (tiles - held)
    mine = pl.multiple_of(core * height, 8)
    other = pl.multiple_of((1 - core) * height, 8)

    def step(index, slot):
        start = start_ref[origin + place + index]
        out_ref[index, pl.ds(mine, height)] = done_ref[index]
        out_ref[index, pl.ds(other, height)] = resampled_tile(
            [got_ref], start, weights_ref[place + index]
        )

    unrolled(step, half)


def resample_rest(group, tiles, start, weights, got, done):
    count, height, _ = done.shape
    return call(
        functools.partial(resample_rest_body, group, tiles),
        [f32(count, 2 * height, LANES)],
        [],
        (start, weights, got, done),
    )[0]


def resample_apart_body(group, tiles, start_ref, weights_ref, sino_ref, got_ref, out_ref, stack):
    held, (first, half) = weights_ref.shape[0], group
    views, rows, _ = sino_ref.shape
    height = views * rows
    _, core = position()
    place = jnp.where(core == 0, first, held - first - half)
    origin = core * (tiles - held)
    mine = pl.multiple_of(core * height, 8)
    other = pl.multiple_of((1 - core) * height, 8)

    def step(index, slot):
        start = start_ref[origin + place + index]
        total = resampled_tile([sino_ref, got_ref], start, weights_ref[place + index])
        stack[slot, pl.ds(mine, height)] = total[:height]
        stack[slot, pl.ds(other, height)] = total[height:]
        for row in range(rows):
            out_ref[index, row] = stack[slot, pl.ds(row, 2 * views, stride=rows), :]

    unrolled(step, half)


def resample_apart(group, tiles, start, weights, sino, got, after):
    views, rows, _ = sino.shape
    return call(
        functools.partial(resample_apart_body, group, tiles),
        [f32(group[1], rows, 2 * views, LANES)],
        [pltpu.VMEM((2, 2 * views * rows + 8, LANES), jnp.float32)],
        (start, weights, sino, got),
        cycles(4000),
        after,
    )[0]


def rows_body(group, tiles, offset_ref, even_ref, odd_ref, own_ref, weights_ref, out_ref, stack):
    count, height, _ = own_ref.shape
    views = height // 2
    _, core = position()
    after = lax.axis_index("row") % 2 == 0
    even_at = pl.multiple_of(jnp.where(after, 2 * height, 0), 8)
    odd_at = pl.multiple_of(jnp.where(after, 0, 2 * height), 8)

    def step(index, slot):
        tile = tile_of(index, group, tiles, core)
        offset = offset_ref[tile]
        stack[slot, pl.ds(even_at, height)] = even_ref[index]
        stack[slot, pl.ds(odd_at, height)] = odd_ref[index]
        stack[slot, height : 2 * height] = own_ref[index]
        weights = weights_ref[:, pl.ds(pl.multiple_of(tile * LANES, LANES), LANES)]

        def picked(row):
            lifted = row + 2
            first = lifted // 2 * height + lifted % 2
            return stack[slot, pl.ds(first, views, stride=2), :]

        terms = [picked(row + offset) for row in range(3)]
        for row in range(2):
            out_ref[index, row] = weights[0:1] * terms[row] + weights[1:2] * terms[row + 1]

    unrolled(step, count)


def interpolate_rows(group, tiles, offset, even, odd, own, weights, after):
    count, height, _ = own.shape
    return call(
        functools.partial(rows_body, group, tiles),
        [f32(count, 2, height // 2, LANES)],
        [pltpu.VMEM((2, 3 * height + 8, LANES), jnp.float32)],
        (offset, even, odd, own, weights),
        after=after,
    )[0]


def last_rows_body(group, tiles, offset_ref, even_ref, odd_ref, own_ref, weights_ref, keep_ref, send_ref, stack):
    count, parts, rows, chip_views, _ = own_ref.shape
    views = chip_views // 2
    _, core = position()
    after = lax.axis_index("row") % 2 == 0
    even_at = jnp.where(after, 2 * rows, 0)
    odd_at = jnp.where(after, 0, 2 * rows)
    mine = pl.multiple_of(core * views, 8)
    other = pl.multiple_of((1 - core) * views, 8)

    def step(index, slot):
        tile = tile_of(index, group, tiles, core)
        first = offset_ref[tile] + rows
        weights = weights_ref[:, pl.ds(pl.multiple_of(tile * LANES, LANES), LANES)]
        for part in range(parts):
            for row in range(rows):
                stack[slot, even_at + row] = even_ref[index, part, row]
                stack[slot, odd_at + row] = odd_ref[index, part, row]
                stack[slot, rows + row] = own_ref[index, part, row]
            for out_ref, begin in ((keep_ref, mine), (send_ref, other)):
                terms = [stack[slot, first + i, pl.ds(begin, views)] for i in range(rows + 1)]
                for row in range(rows):
                    out_ref[index, part, row] = weights[0:1] * terms[row] + weights[1:2] * terms[row + 1]

    unrolled(step, count)


def interpolate_rows_last(group, tiles, offset, even, odd, own, weights):
    count, parts, rows, chip_views, _ = own.shape
    return call(
        functools.partial(last_rows_body, group, tiles),
        [f32(count, parts, rows, chip_views // 2, LANES)] * 2,
        [pltpu.VMEM((2, 3 * rows, chip_views, LANES), jnp.float32)],
        (offset, even, odd, own, weights),
        cycles(4000),
    )


def select_body(group, tiles, view_ref, conj_ref, own_ref, got_ref, out_ref, stack):
    count, rows, chip_views, lanes = own_ref.shape
    side, core = position()

    def shifts(index):
        tile = tile_of(index, group, tiles, core)
        shift = view_ref[tile]
        return shift, shift + conj_ref[tiles - 1 - tile]

    def slots(low, high):
        return low + lax.broadcasted_iota(jnp.int32, (high - low, lanes), 0)

    def across_x(index, slot):
        shift, opposite = shifts(index)
        own_at = pl.multiple_of((1 - side) * chip_views, 8)
        got_at = pl.multiple_of(side * chip_views, 8)
        for row in range(rows):
            out = out_ref.at[index, row]
            both = stack.at[slot, row]
            both[pl.ds(own_at, chip_views)] = own_ref[index, row]
            both[pl.ds(got_at, chip_views)] = got_ref[index, row]
            out[0:32] = jnp.where(slots(0, 32) >= shift + 32, both[96:128], both[0:32])
            out[32:80] = jnp.where(slots(0, 48) >= opposite + 48, both[16:64], both[64:112])
            out[80:88] = jnp.zeros((8, lanes), jnp.float32)

    def across_y_first(index, slot):
        shift, opposite = shifts(index)
        for row in range(rows):
            out = out_ref.at[index, row]
            both = stack.at[slot, row]
            both[0:64] = own_ref[index, row]
            both[64:128] = got_ref[index, row]
            out[0:40] = jnp.where(slots(0, 40) >= opposite, both[0:40], both[72:112])
            out[40:56] = both[40:56]
            out[56:72] = jnp.where(slots(56, 72) >= 88 + shift, both[96:112], both[56:72])
            out[72:88] = both[112:128]

    def across_y_last(index, slot):
        shift, opposite = shifts(index)
        for row in range(rows):
            out = out_ref.at[index, row]
            both = stack.at[slot, row]
            both[0:64] = got_ref[index, row]
            both[64:128] = own_ref[index, row]
            out[0:16] = both[0:16]
            out[16:32] = jnp.where(slots(16, 32) < shift + 3, both[16:32], both[56:72])
            out[32:48] = both[72:88]
            out[48:88] = jnp.where(slots(48, 88) < 91 + opposite, both[88:128], both[16:56])

    pl.when(core == 0)(lambda: unrolled(across_x, count))
    pl.when((core == 1) & (side == 0))(lambda: unrolled(across_y_first, count))
    pl.when((core == 1) & (side == 1))(lambda: unrolled(across_y_last, count))


def select_views(group, tiles, view_offset, conj_offset, own, got, after=()):
    count, rows, chip_views, _ = own.shape
    return call(
        functools.partial(select_body, group, tiles),
        [f32(count, rows, SLOTS, LANES)],
        [pltpu.VMEM((2, rows, 2 * chip_views, LANES), jnp.float32)],
        (view_offset, conj_offset, own, got),
        after=after,
    )[0]


def views_body(group, tiles, exchanged, view_ref, conj_ref, weights_ref, *refs):
    *blocks, stack = refs
    outs = blocks[3 if exchanged else 6 :]
    blocks = blocks[: 3 if exchanged else 6]
    count, _, rows, views, _ = outs[0].shape
    side, core = position()
    firsts = (core, 1 - core) if len(outs) == 2 else (0,)
    taps = weights_ref.shape[0]

    def interpolate(index, slot, row):
        tile = tile_of(index, group, tiles, core)
        weights = weights_ref[:, pl.ds(pl.multiple_of(tile * LANES, LANES), LANES)]
        shift = view_ref[tile]
        opposite = shift + conj_ref[tiles - 1 - tile]
        for part, by in ((0, 32 + shift), (1, 176 + opposite)):
            for out_ref, first in zip(outs, firsts):
                begin = by + first * views
                total = weights[0:1] * stack[slot, row, pl.ds(begin, views)]
                for tap in range(1, taps):
                    total = total + weights[tap : tap + 1] * stack[slot, row, pl.ds(begin + tap, views)]
                out_ref[index, part, row] = total

    def run(parts):
        def step(index, slot):
            for row in range(rows):
                at = 0
                for part in parts(*(ref.at[index, row] for ref in blocks)):
                    stack[slot, row, at : at + part.shape[0]] = part[...]
                    at += part.shape[0]
                interpolate(index, slot, row)

        unrolled(step, count)

    def from_neighbours(before, own, after, early, middle, late):
        return before, own, after, early, middle, late

    def from_x(own, beyond, got):
        near, far = got.at[0:32], got.at[32:80]
        return near, own, near, far, beyond, far

    def from_y_first(own, beside, got):
        return got.at[56:88], own, beside.at[0:32], beside.at[16:64], got.at[0:72], got.at[0:40]

    def from_y_last(own, beside, got):
        return beside.at[32:64], own, got.at[0:32], got.at[48:88], got.at[16:88], beside.at[0:48]

    if exchanged:
        pl.when(core == 0)(lambda: run(from_x))
        pl.when((core == 1) & (side == 0))(lambda: run(from_y_first))
        pl.when((core == 1) & (side == 1))(lambda: run(from_y_last))
    else:
        run(from_neighbours)


def interpolate_views(group, tiles, exchanged, view_offset, conj_offset, weights, blocks, pieces, cost=SHORT, after=()):
    count, rows, chip_views, _ = blocks[0 if exchanged else 1].shape
    return call(
        functools.partial(views_body, group, tiles, exchanged),
        [f32(count, 2, rows, chip_views // pieces, LANES)] * pieces,
        [pltpu.VMEM((2, rows, 288, LANES), jnp.float32)],
        (view_offset, conj_offset, weights, *blocks),
        cost,
        after,
    )


def ramp(lag):
    lag = lag.astype(np.float64)
    odd = np.abs(lag) % 2 == 1
    values = np.where(lag == 0, 0.25, np.where(odd, -1.0 / (math.pi**2 * np.maximum(lag * lag, 1.0)), 0.0))
    return np.where(np.abs(lag) <= KR, values, 0.0).astype(np.float32)


def filter_matrix():
    column = np.arange(WINDOW)[:, None]
    place = np.arange(2 * LANES)[None, :]
    lag = place - 2 * (column - LANES)
    whole = np.concatenate([ramp(lag), ramp(lag - 1)[::-1]], axis=0)
    high = whole.astype(jnp.bfloat16)
    low = (whole - high.astype(np.float32)).astype(jnp.bfloat16)
    return jnp.asarray(high), jnp.asarray(low)


def stage_spans(groups, number, tiles):
    first, half = groups[number]
    begin = first - 1 if number else 0
    if number == len(groups) - 1:
        ranges = [(begin, tiles - begin)]
    else:
        ranges = [(begin, first + half - 1), (tiles - first - half + 1, tiles - begin)]
    spans = []
    for low, high in ranges:
        while low < high:
            count = min(4, high - low)
            spans.append((low, count))
            low += count
    return spans


def filter_body(groups, number, tiles, high_ref, low_ref, *refs):
    parts = refs[: 4 if number else 2]
    out_any, mixed, high_all, low_all, result, sems = refs[-6:]
    views = out_any.shape[0]
    _, core = position()
    if number == 0:
        for ref in (high_all, low_all):
            for part in range(2):
                ref[part, 0] = jnp.zeros(ref.shape[2:], ref.dtype)
                ref[part, tiles + 1] = jnp.zeros(ref.shape[2:], ref.dtype)

    def gather(group, ref, owner, index, slot):
        tile = tile_of(index, group, tiles, owner)
        for part in range(2):
            for row in range(2):
                mixed[slot, part, pl.ds(row, views, stride=2), :] = ref[index, part, row]
            high, low = split(mixed[slot, part, 0 : 2 * views])
            high_all[part, tile + 1] = high
            low_all[part, tile + 1] = low

    for ref, owner in zip(parts[:2], (core, 1 - core)):
        unrolled(functools.partial(gather, groups[number], ref, owner), groups[number][1])
    if number:
        half = groups[number - 1][1]
        for ref, owner in zip(parts[2:], (core, 1 - core)):
            begin = jnp.where(owner == 0, half - 2, 0)
            for i in range(2):
                gather(groups[number - 1], ref, owner, begin + i, i)

    copies = []
    for place, (first, count) in enumerate(stage_spans(groups, number, tiles)):

        def window(ref):
            pieces = []
            for section in range(3):
                piece = ref[0, first + section : first + section + count]
                pieces.append(piece.reshape(count * 2 * views, LANES))
            for section in range(3):
                last = tiles - 1 - first + section
                piece = jnp.stack([ref[1, last - i] for i in range(count)])
                pieces.append(piece.reshape(count * 2 * views, LANES))
            return jnp.concatenate(pieces, axis=1)

        high, low = window(high_all), window(low_all)
        total = dot_terms(high, low, high_ref[...]) + dot(high, low_ref[...])
        for i in range(count):
            block = total[2 * views * i : 2 * views * (i + 1)].reshape(views, 2, 2 * LANES)
            result[:, :, (first + i) * 2 * LANES : (first + i + 1) * 2 * LANES] = block
        columns = pl.ds(first * 2 * LANES, count * 2 * LANES)
        copy = pltpu.make_async_copy(
            result.at[:, :, columns], out_any.at[:, :, columns], sems.at[place]
        )
        copy.start()
        copies.append(copy)
    for copy in copies:
        copy.wait()


def ramp_filter(groups, number, tiles, keeps, gots, out):
    views = keeps[0].shape[3]
    args = [*filter_matrix(), keeps[number], gots[number]]
    if number:
        args += [keeps[number - 1], gots[number - 1], out]
    stored = pltpu.VMEM((2, tiles + 2, 2 * views, LANES), jnp.bfloat16)
    shape = f32(views, 2, 2 * tiles * LANES)
    return call(
        functools.partial(filter_body, groups, number, tiles),
        [shape],
        [
            pltpu.VMEM((2, 2, 2 * views + 8, LANES), jnp.float32),
            stored,
            stored,
            pltpu.VMEM(shape.shape, jnp.float32),
            pltpu.SemaphoreType.DMA((len(stage_spans(groups, number, tiles)),)),
        ],
        args,
        specs=[VMEM] * 6 + [ANY] if number else [VMEM] * 4,
        out=ANY,
        aliases={6: 0} if number else {},
        cost=SHORT if number else cycles(6000),
    )[0]


def permuted(value, axis, target):
    count = lax.axis_size(axis)
    pairs = [(i, target(i)) for i in range(count)]
    return lax.ppermute(value, axis, [(i, j) for i, j in pairs if 0 <= j < count])


def swapped(value):
    return permuted(value, "ang", lambda i: i ^ 1)


def row_pairs(own):
    even = permuted(own, "row", lambda i: i ^ 1)
    odd = permuted(own, "row", lambda i: ((i + 1) ^ 1) - 1)
    return even, odd


def first_exchange(own):
    if lax.axis_size("ang") == 8:
        return [permuted(own, "ang", lambda i: i ^ (2 if i % 2 else 4))]
    return []


def second_exchange(own, first, chosen):
    devices = lax.axis_size("ang")
    if first:
        return [own, *first, permuted(chosen[0], "ang", lambda i: i ^ (4 if i % 2 else 2))]

    def ahead(begin, end, chips):
        return permuted(own[:, :, begin:end], "ang", lambda i: (i - 2 * chips) % devices)

    turned = devices // 4
    return [
        ahead(32, 64, -1),
        own,
        ahead(0, 32, 1),
        ahead(16, 64, turned - 1),
        ahead(0, 64, turned),
        ahead(0, 48, turned + 1),
    ]


def on_device(
    sinogram, col_weights, col_start, view_offset, row_offset, conj_offset, ang_weights, row_weights
):
    tiles = col_weights.shape[0]
    exchanged = lax.axis_size("ang") == 8
    offsets = (view_offset, conj_offset)
    groups = (OUTER, INNER)

    beside = swapped(sinogram)
    inner, weights, sino = resample_own(INNER, col_start, col_weights, sinogram)
    inner = resample_rest(INNER, tiles, col_start, weights, beside, inner)
    inner_halo = row_pairs(inner)
    outer = resample_apart(OUTER, tiles, col_start, weights, sino, beside, (inner,))

    first = first_exchange(outer)
    chosen = [select_views(OUTER, tiles, *offsets, outer, got) for got in first]
    parts = second_exchange(outer, first, chosen)
    (outer,) = interpolate_views(
        OUTER, tiles, exchanged, *offsets, ang_weights, parts, 1, cycles(5000)
    )
    outer_halo = row_pairs(outer)

    inner = interpolate_rows(INNER, tiles, row_offset, *inner_halo, inner, row_weights, chosen)
    first = first_exchange(inner)
    chosen = [select_views(INNER, tiles, *offsets, inner, got, (outer,)) for got in first]
    parts = second_exchange(inner, first, chosen)

    outer_keep, send = interpolate_rows_last(
        OUTER, tiles, row_offset, *outer_halo, outer, row_weights
    )
    outer_got = swapped(send)
    out = ramp_filter(groups, 0, tiles, [outer_keep], [outer_got], None)
    inner_keep, send = interpolate_views(
        INNER, tiles, exchanged, *offsets, ang_weights, parts, 2
    )
    inner_got = swapped(send)
    return ramp_filter(
        groups, 1, tiles, (outer_keep, inner_keep), (outer_got, inner_got), out
    )


def solution(mesh):
    return jax.shard_map(
        on_device,
        mesh=mesh,
        in_specs=(P("ang", "row", None), P(), P(), P(), P(), P(), P(), P()),
        out_specs=P("ang", "row", None),
        check_vma=False,
    )
```

```python
import functools
import math

import jax
import jax.numpy as jnp
import numpy as np
from jax import lax
from jax.experimental import pallas as pl
from jax.experimental.pallas import tpu as pltpu
from jax.sharding import PartitionSpec as P

KR = 256
OUTER, INNER = (0, 6), (6, 10)
LANES = 128
WINDOW = 3 * LANES
SLOTS = 88
VMEM = pl.BlockSpec(memory_space=pltpu.VMEM)
SMEM = pl.BlockSpec(memory_space=pltpu.SMEM)
ANY = pl.BlockSpec(memory_space=pl.ANY)
SHORT = pl.CostEstimate(flops=1, bytes_accessed=1, transcendentals=0)


def cycles(number):
    return pl.CostEstimate(flops=number << 19, bytes_accessed=1, transcendentals=0)


def call(body, outs, scratch, args, cost=SHORT, after=(), specs=None, limit=48, out=VMEM, aliases={}):
    if specs is None:
        specs = [SMEM if a.dtype == jnp.int32 else VMEM for a in args]
    taken = len(args)

    def kernel(*refs):
        body(*refs[:taken], *refs[taken + len(after) :])

    return pl.pallas_call(
        kernel,
        out_shape=outs,
        in_specs=[*specs, *[ANY] * len(after)],
        out_specs=[out] * len(outs),
        scratch_shapes=scratch,
        input_output_aliases=aliases,
        compiler_params=pltpu.CompilerParams(vmem_limit_bytes=limit << 20),
        cost_estimate=cost,
    )(*args, *after)


def hbm(x):
    return pltpu.with_memory_space_constraint(x, pltpu.HBM)


def f32(*shape):
    return jax.ShapeDtypeStruct(shape, jnp.float32)


def position():
    index = lax.axis_index("ang")
    return index // 2 % 2, index % 2


def tile_of(index, group, tiles, core):
    first, half = group
    return index + jnp.where(core == 0, first, tiles - first - half)


def split(x):
    high = x.astype(jnp.bfloat16)
    low = (x - high.astype(jnp.float32)).astype(jnp.bfloat16)
    return high, low


def dot(a, b):
    return jnp.dot(a, b, preferred_element_type=jnp.float32)


def dot_terms(high, low, b):
    both = dot(jnp.concatenate([high, low], axis=0), b)
    return both[: high.shape[0]] + both[high.shape[0] :]


def unrolled(step, count):
    for index in range(count):
        step(index, index % 2)


def paired(step, count):
    def pair(index, carry):
        step(2 * index, 0)
        step(2 * index + 1, 1)
        return carry

    lax.fori_loop(0, count // 2, pair, 0)
    if count % 2:
        step(count - 1, 0)


def resampled_tile(slab_refs, start, weights):
    cols = slab_refs[0].shape[2]
    base = jnp.minimum(start // LANES * LANES, cols - WINDOW)
    columns = pl.ds(pl.multiple_of(base, LANES), WINDOW)
    slabs = [ref[:, :, columns].reshape(-1, WINDOW) for ref in slab_refs]
    slab = jnp.concatenate(slabs, axis=0)
    slab = pltpu.roll(slab, WINDOW - (start - base), 1)[:, : weights.shape[0]]
    return dot_terms(*split(slab), weights)


def resample_own_body(group, start_any, weights_any, sino_any, out_ref, weights_ref, sino_ref, start_ref, sems):
    tiles = weights_any.shape[0]
    held = weights_ref.shape[0]
    first, half = group
    _, core = position()
    place = jnp.where(core == 0, first, held - first - half)
    origin = core * (tiles - held)
    later = jnp.where(core == 0, 0, half)
    needed = [
        pltpu.make_async_copy(start_any, start_ref, sems.at[0]),
        pltpu.make_async_copy(sino_any, sino_ref, sems.at[1]),
        pltpu.make_async_copy(
            weights_any.at[pl.ds(origin + place, half)], weights_ref.at[pl.ds(place, half)], sems.at[2]
        ),
    ]
    rest = pltpu.make_async_copy(
        weights_any.at[pl.ds(origin + later, held - half)],
        weights_ref.at[pl.ds(later, held - half)],
        sems.at[3],
    )
    for copy in (*needed, rest):
        copy.start()
    for copy in needed:
        copy.wait()

    def step(index, slot):
        start = start_ref[origin + place + index]
        out_ref[index] = resampled_tile([sino_ref], start, weights_ref[place + index])

    unrolled(step, half)
    rest.wait()


def resample_own(group, start, weights, sino):
    views, rows, _ = sino.shape
    held = weights.shape[0] // 2
    return call(
        functools.partial(resample_own_body, group),
        [
            f32(group[1], views * rows, LANES),
            jax.ShapeDtypeStruct((held, *weights.shape[1:]), weights.dtype),
            f32(*sino.shape),
        ],
        [pltpu.SMEM(start.shape, jnp.int32), pltpu.SemaphoreType.DMA((4,))],
        [hbm(x) for x in (start, weights, sino)],
        specs=[ANY] * 3,
    )


def resample_rest_body(group, tiles, start_ref, weights_ref, got_ref, done_ref, out_ref):
    held, (first, half) = weights_ref.shape[0], group
    height = done_ref.shape[1]
    _, core = position()
    place = jnp.where(core == 0, first, held - first - half)
    origin = core * (tiles - held)
    mine = pl.multiple_of(core * height, 8)
    other = pl.multiple_of((1 - core) * height, 8)

    def step(index, slot):
        start = start_ref[origin + place + index]
        out_ref[index, pl.ds(mine, height)] = done_ref[index]
        out_ref[index, pl.ds(other, height)] = resampled_tile(
            [got_ref], start, weights_ref[place + index]
        )

    unrolled(step, half)


def resample_rest(group, tiles, start, weights, got, done):
    count, height, _ = done.shape
    return call(
        functools.partial(resample_rest_body, group, tiles),
        [f32(count, 2 * height, LANES)],
        [],
        (start, weights, got, done),
    )[0]


def resample_apart_body(group, tiles, start_ref, weights_ref, sino_ref, got_ref, out_ref, stack):
    held, (first, half) = weights_ref.shape[0], group
    views, rows, _ = sino_ref.shape
    height = views * rows
    _, core = position()
    place = jnp.where(core == 0, first, held - first - half)
    origin = core * (tiles - held)
    mine = pl.multiple_of(core * height, 8)
    other = pl.multiple_of((1 - core) * height, 8)

    def step(index, slot):
        start = start_ref[origin + place + index]
        total = resampled_tile([sino_ref, got_ref], start, weights_ref[place + index])
        stack[slot, pl.ds(mine, height)] = total[:height]
        stack[slot, pl.ds(other, height)] = total[height:]
        for row in range(rows):
            out_ref[index, row] = stack[slot, pl.ds(row, 2 * views, stride=rows), :]

    unrolled(step, half)


def resample_apart(group, tiles, start, weights, sino, got, after):
    views, rows, _ = sino.shape
    return call(
        functools.partial(resample_apart_body, group, tiles),
        [f32(group[1], rows, 2 * views, LANES)],
        [pltpu.VMEM((2, 2 * views * rows + 8, LANES), jnp.float32)],
        (start, weights, sino, got),
        cycles(4000),
        after,
    )[0]


def rows_body(group, tiles, offset_ref, odd_ref, even_ref, own_ref, weights_ref, out_ref):
    count, height, _ = own_ref.shape
    views = height // 2
    _, core = position()

    def run(before, after):
        def step(index, slot):
            tile = tile_of(index, group, tiles, core)
            offset = offset_ref[tile]
            weights = weights_ref[:, pl.ds(pl.multiple_of(tile * LANES, LANES), LANES)]
            lines = [
                ref[index, pl.ds(row, views, stride=2), :]
                for ref in (before, own_ref, after)
                for row in range(2)
            ]
            terms = []
            for row in range(3):
                low = jnp.where(offset == -2, lines[row], lines[row + 1])
                high = jnp.where(offset == 0, lines[row + 2], lines[row + 3])
                terms.append(jnp.where(offset < 0, low, high))
            for row in range(2):
                out_ref[index, row] = weights[0:1] * terms[row] + weights[1:2] * terms[row + 1]

        unrolled(step, count)

    beside = lax.axis_index("row") % 2
    pl.when(beside == 0)(lambda: run(odd_ref, even_ref))
    pl.when(beside == 1)(lambda: run(even_ref, odd_ref))


def interpolate_rows(group, tiles, offset, even, odd, own, weights, after):
    count, height, _ = own.shape
    return call(
        functools.partial(rows_body, group, tiles),
        [f32(count, 2, height // 2, LANES)],
        [],
        (offset, odd, even, own, weights),
        after=after,
    )[0]


def last_rows_body(group, tiles, offset_ref, odd_ref, even_ref, own_ref, weights_ref, keep_ref, send_ref, stack):
    count, parts, rows, chip_views, _ = own_ref.shape
    views = chip_views // 2
    _, core = position()
    after = lax.axis_index("row") % 2 == 0
    even_at = jnp.where(after, 2 * rows, 0)
    odd_at = jnp.where(after, 0, 2 * rows)
    mine = pl.multiple_of(core * views, 8)
    other = pl.multiple_of((1 - core) * views, 8)

    def step(index, slot):
        tile = tile_of(index, group, tiles, core)
        first = offset_ref[tile] + rows
        weights = weights_ref[:, pl.ds(pl.multiple_of(tile * LANES, LANES), LANES)]
        for part in range(parts):
            for row in range(rows):
                stack[slot, even_at + row] = even_ref[index, part, row]
                stack[slot, odd_at + row] = odd_ref[index, part, row]
                stack[slot, rows + row] = own_ref[index, part, row]
            for out_ref, begin in ((keep_ref, mine), (send_ref, other)):
                terms = [stack[slot, first + i, pl.ds(begin, views)] for i in range(rows + 1)]
                for row in range(rows):
                    out_ref[index, part, row] = weights[0:1] * terms[row] + weights[1:2] * terms[row + 1]

    unrolled(step, count)


def interpolate_rows_last(group, tiles, offset, even, odd, own, weights):
    count, parts, rows, chip_views, _ = own.shape
    return call(
        functools.partial(last_rows_body, group, tiles),
        [f32(count, parts, rows, chip_views // 2, LANES)] * 2,
        [pltpu.VMEM((2, 3 * rows, chip_views, LANES), jnp.float32)],
        (offset, odd, even, own, weights),
        cycles(4000),
    )


def select_body(group, tiles, view_ref, conj_ref, own_ref, got_ref, out_ref):
    count, rows, chip_views, lanes = own_ref.shape
    side, core = position()

    def shifts(index):
        tile = tile_of(index, group, tiles, core)
        shift = view_ref[tile]
        return shift, shift + conj_ref[tiles - 1 - tile]

    def slots(low, high):
        return low + lax.broadcasted_iota(jnp.int32, (high - low, lanes), 0)

    def joined(low, high, first, last):
        if last <= 64:
            return low[first:last]
        if first >= 64:
            return high[first - 64 : last - 64]
        return jnp.concatenate([low[first:64], high[0 : last - 64]], axis=0)

    def across_x(index, row, low, high):
        shift, opposite = shifts(index)
        out = out_ref.at[index, row]
        both = functools.partial(joined, low.at[index, row], high.at[index, row])
        out[0:32] = jnp.where(slots(0, 32) >= shift + 32, both(96, 128), both(0, 32))
        out[32:80] = jnp.where(slots(0, 48) >= opposite + 48, both(16, 64), both(64, 112))
        out[80:88] = jnp.zeros((8, lanes), jnp.float32)

    def across_y_first(index, row, low, high):
        shift, opposite = shifts(index)
        out = out_ref.at[index, row]
        both = functools.partial(joined, low.at[index, row], high.at[index, row])
        out[0:40] = jnp.where(slots(0, 40) >= opposite, both(0, 40), both(72, 112))
        out[40:56] = both(40, 56)
        out[56:72] = jnp.where(slots(56, 72) >= 88 + shift, both(96, 112), both(56, 72))
        out[72:88] = both(112, 128)

    def across_y_last(index, row, low, high):
        shift, opposite = shifts(index)
        out = out_ref.at[index, row]
        both = functools.partial(joined, low.at[index, row], high.at[index, row])
        out[0:16] = both(0, 16)
        out[16:32] = jnp.where(slots(16, 32) < shift + 3, both(16, 32), both(56, 72))
        out[32:48] = both(72, 88)
        out[48:88] = jnp.where(slots(48, 88) < 91 + opposite, both(88, 128), both(16, 56))

    def run(part, low, high):
        for index in range(count):
            for row in range(rows):
                part(index, row, low, high)

    pl.when((core == 0) & (side == 0))(lambda: run(across_x, got_ref, own_ref))
    pl.when((core == 0) & (side == 1))(lambda: run(across_x, own_ref, got_ref))
    pl.when((core == 1) & (side == 0))(lambda: run(across_y_first, own_ref, got_ref))
    pl.when((core == 1) & (side == 1))(lambda: run(across_y_last, got_ref, own_ref))


def select_views(group, tiles, view_offset, conj_offset, own, got, after=()):
    count, rows, chip_views, _ = own.shape
    return call(
        functools.partial(select_body, group, tiles),
        [f32(count, rows, SLOTS, LANES)],
        [],
        (view_offset, conj_offset, own, got),
        after=after,
    )[0]


def views_body(group, tiles, exchanged, view_ref, conj_ref, weights_ref, *refs):
    *blocks, stack = refs
    outs = blocks[3 if exchanged else 6 :]
    blocks = blocks[: 3 if exchanged else 6]
    count, _, rows, views, _ = outs[0].shape
    side, core = position()
    firsts = (core, 1 - core) if len(outs) == 2 else (0,)
    taps = weights_ref.shape[0]

    def interpolate(index, slot, row):
        tile = tile_of(index, group, tiles, core)
        weights = weights_ref[:, pl.ds(pl.multiple_of(tile * LANES, LANES), LANES)]
        shift = view_ref[tile]
        opposite = shift + conj_ref[tiles - 1 - tile]
        for part, by in ((0, 32 + shift), (1, 176 + opposite)):
            for out_ref, first in zip(outs, firsts):
                begin = by + first * views
                total = weights[0:1] * stack[slot, row, pl.ds(begin, views)]
                for tap in range(1, taps):
                    total = total + weights[tap : tap + 1] * stack[slot, row, pl.ds(begin + tap, views)]
                out_ref[index, part, row] = total

    def run(parts):
        def step(index, slot):
            for row in range(rows):
                at = 0
                for part in parts(*(ref.at[index, row] for ref in blocks)):
                    stack[slot, row, at : at + part.shape[0]] = part[...]
                    at += part.shape[0]
                interpolate(index, slot, row)

        unrolled(step, count)

    def from_neighbours(before, own, after, early, middle, late):
        return before, own, after, early, middle, late

    def from_x(own, beyond, got):
        near, far = got.at[0:32], got.at[32:80]
        return near, own, near, far, beyond, far

    def from_y_first(own, beside, got):
        return got.at[56:88], own, beside.at[0:32], beside.at[16:64], got.at[0:72], got.at[0:40]

    def from_y_last(own, beside, got):
        return beside.at[32:64], own, got.at[0:32], got.at[48:88], got.at[16:88], beside.at[0:48]

    if exchanged:
        pl.when(core == 0)(lambda: run(from_x))
        pl.when((core == 1) & (side == 0))(lambda: run(from_y_first))
        pl.when((core == 1) & (side == 1))(lambda: run(from_y_last))
    else:
        run(from_neighbours)


def interpolate_views(group, tiles, exchanged, view_offset, conj_offset, weights, blocks, pieces, cost=SHORT, after=()):
    count, rows, chip_views, _ = blocks[0 if exchanged else 1].shape
    return call(
        functools.partial(views_body, group, tiles, exchanged),
        [f32(count, 2, rows, chip_views // pieces, LANES)] * pieces,
        [pltpu.VMEM((2, rows, 288, LANES), jnp.float32)],
        (view_offset, conj_offset, weights, *blocks),
        cost,
        after,
    )


def ramp(lag):
    lag = lag.astype(np.float64)
    odd = np.abs(lag) % 2 == 1
    values = np.where(lag == 0, 0.25, np.where(odd, -1.0 / (math.pi**2 * np.maximum(lag * lag, 1.0)), 0.0))
    return np.where(np.abs(lag) <= KR, values, 0.0).astype(np.float32)


def filter_matrix():
    column = np.arange(WINDOW)[:, None]
    place = np.arange(2 * LANES)[None, :]
    lag = place - 2 * (column - LANES)
    whole = np.concatenate([ramp(lag), ramp(lag - 1)[::-1]], axis=0)
    high = whole.astype(jnp.bfloat16)
    low = (whole - high.astype(np.float32)).astype(jnp.bfloat16)
    return jnp.asarray(high), jnp.asarray(low)


def stage_spans(groups, number, tiles):
    first, half = groups[number]
    begin = first - 1 if number else 0
    if number == len(groups) - 1:
        ranges = [(begin, tiles - begin)]
    else:
        ranges = [(begin, first + half - 1), (tiles - first - half + 1, tiles - begin)]
    spans = []
    for low, high in ranges:
        while low < high:
            count = min(4, high - low)
            spans.append((low, count))
            low += count
    return spans


def filter_body(groups, number, tiles, high_ref, low_ref, *refs):
    parts = refs[: 4 if number else 2]
    if number:
        earlier, out_any, mixed, high_all, low_all, result, sems = refs[4:]
    else:
        result, mixed, high_all, low_all = refs[2:]
    views = result.shape[0]
    _, core = position()
    if number == 0:
        for ref in (high_all, low_all):
            for part in range(2):
                ref[part, 0] = jnp.zeros(ref.shape[2:], ref.dtype)
                ref[part, tiles + 1] = jnp.zeros(ref.shape[2:], ref.dtype)

    def gather(group, ref, owner, index, slot):
        tile = tile_of(index, group, tiles, owner)
        for part in range(2):
            for row in range(2):
                mixed[slot, part, pl.ds(row, views, stride=2), :] = ref[index, part, row]
            high, low = split(mixed[slot, part, 0 : 2 * views])
            high_all[part, tile + 1] = high
            low_all[part, tile + 1] = low

    for ref, owner in zip(parts[:2], (core, 1 - core)):
        unrolled(functools.partial(gather, groups[number], ref, owner), groups[number][1])
    if number:
        half = groups[number - 1][1]
        for ref, owner in zip(parts[2:], (core, 1 - core)):
            begin = jnp.where(owner == 0, half - 2, 0)
            for i in range(2):
                gather(groups[number - 1], ref, owner, begin + i, i)

    copies = []

    def leave(source, first, count):
        columns = pl.ds(first * 2 * LANES, count * 2 * LANES)
        copies.append(
            pltpu.make_async_copy(source.at[:, :, columns], out_any.at[:, :, columns], sems.at[len(copies)])
        )
        copies[-1].start()

    if number:
        for first, count in stage_spans(groups, 0, tiles):
            leave(earlier, first, count)
    for first, count in stage_spans(groups, number, tiles):

        def window(ref):
            pieces = []
            for section in range(3):
                piece = ref[0, first + section : first + section + count]
                pieces.append(piece.reshape(count * 2 * views, LANES))
            for section in range(3):
                last = tiles - 1 - first + section
                piece = jnp.stack([ref[1, last - i] for i in range(count)])
                pieces.append(piece.reshape(count * 2 * views, LANES))
            return jnp.concatenate(pieces, axis=1)

        high, low = window(high_all), window(low_all)
        total = dot_terms(high, low, high_ref[...]) + dot(high, low_ref[...])
        for i in range(count):
            block = total[2 * views * i : 2 * views * (i + 1)].reshape(views, 2, 2 * LANES)
            result[:, :, (first + i) * 2 * LANES : (first + i + 1) * 2 * LANES] = block
        if number:
            leave(result, first, count)
    for copy in copies:
        copy.wait()


def ramp_filter(groups, number, tiles, keeps, gots, out):
    views = keeps[0].shape[3]
    args = [*filter_matrix(), keeps[number], gots[number]]
    stored = pltpu.VMEM((2, tiles + 2, 2 * views, LANES), jnp.bfloat16)
    scratch = [pltpu.VMEM((2, 2, 2 * views + 8, LANES), jnp.float32), stored, stored]
    shape = f32(views, 2, 2 * tiles * LANES)
    if number:
        args += [keeps[number - 1], gots[number - 1], out]
        spans = sum(len(stage_spans(groups, i, tiles)) for i in range(2))
        scratch += [pltpu.VMEM(shape.shape, jnp.float32), pltpu.SemaphoreType.DMA((spans,))]
    return call(
        functools.partial(filter_body, groups, number, tiles),
        [shape],
        scratch,
        args,
        out=ANY if number else VMEM,
        cost=SHORT if number else cycles(6000),
    )[0]


def permuted(value, axis, target):
    count = lax.axis_size(axis)
    pairs = [(i, target(i)) for i in range(count)]
    return lax.ppermute(value, axis, [(i, j) for i, j in pairs if 0 <= j < count])


def swapped(value):
    return permuted(value, "ang", lambda i: i ^ 1)


def row_pairs(own):
    even = permuted(own, "row", lambda i: i ^ 1)
    odd = permuted(own, "row", lambda i: ((i + 1) ^ 1) - 1)
    return even, odd


def first_exchange(own):
    if lax.axis_size("ang") == 8:
        return [permuted(own, "ang", lambda i: i ^ (2 if i % 2 else 4))]
    return []


def second_exchange(own, first, chosen):
    devices = lax.axis_size("ang")
    if first:
        return [own, *first, permuted(chosen[0], "ang", lambda i: i ^ (4 if i % 2 else 2))]

    def ahead(begin, end, chips):
        return permuted(own[:, :, begin:end], "ang", lambda i: (i - 2 * chips) % devices)

    turned = devices // 4
    return [
        ahead(32, 64, -1),
        own,
        ahead(0, 32, 1),
        ahead(16, 64, turned - 1),
        ahead(0, 64, turned),
        ahead(0, 48, turned + 1),
    ]


def on_device(
    sinogram, col_weights, col_start, view_offset, row_offset, conj_offset, ang_weights, row_weights
):
    tiles = col_weights.shape[0]
    exchanged = lax.axis_size("ang") == 8
    offsets = (view_offset, conj_offset)
    groups = (OUTER, INNER)

    beside = swapped(sinogram)
    inner, weights, sino = resample_own(INNER, col_start, col_weights, sinogram)
    inner = resample_rest(INNER, tiles, col_start, weights, beside, inner)
    inner_halo = row_pairs(inner)
    outer = resample_apart(OUTER, tiles, col_start, weights, sino, beside, (inner,))

    first = first_exchange(outer)
    chosen = [select_views(OUTER, tiles, *offsets, outer, got) for got in first]
    parts = second_exchange(outer, first, chosen)
    (outer,) = interpolate_views(
        OUTER, tiles, exchanged, *offsets, ang_weights, parts, 1, cycles(5000)
    )
    outer_halo = row_pairs(outer)

    inner = interpolate_rows(INNER, tiles, row_offset, *inner_halo, inner, row_weights, chosen)
    first = first_exchange(inner)
    chosen = [select_views(INNER, tiles, *offsets, inner, got, (outer,)) for got in first]
    parts = second_exchange(inner, first, chosen)

    outer_keep, send = interpolate_rows_last(
        OUTER, tiles, row_offset, *outer_halo, outer, row_weights
    )
    outer_got = swapped(send)
    out = ramp_filter(groups, 0, tiles, [outer_keep], [outer_got], None)
    inner_keep, send = interpolate_views(
        INNER, tiles, exchanged, *offsets, ang_weights, parts, 2
    )
    inner_got = swapped(send)
    return ramp_filter(
        groups, 1, tiles, (outer_keep, inner_keep), (outer_got, inner_got), out
    )


def solution(mesh):
    return jax.shard_map(
        on_device,
        mesh=mesh,
        in_specs=(P("ang", "row", None), P(), P(), P(), P(), P(), P(), P()),
        out_specs=P("ang", "row", None),
        check_vma=False,
    )
```

```python
import functools
import math

import jax
import jax.numpy as jnp
import numpy as np
from jax import lax
from jax.experimental import pallas as pl
from jax.experimental.pallas import tpu as pltpu
from jax.sharding import PartitionSpec as P

KR = 256
LAST_COST = 1
GROUPS = ((0, 5), (5, 6), (11, 5))
LANES = 128
WINDOW = 3 * LANES
SLOTS = 88
VMEM = pl.BlockSpec(memory_space=pltpu.VMEM)
SMEM = pl.BlockSpec(memory_space=pltpu.SMEM)
ANY = pl.BlockSpec(memory_space=pl.ANY)
SHORT = pl.CostEstimate(flops=1, bytes_accessed=1, transcendentals=0)


def cycles(number):
    return pl.CostEstimate(flops=number << 19, bytes_accessed=1, transcendentals=0)


def call(body, outs, scratch, args, cost=SHORT, after=(), specs=None, limit=48, out=VMEM, aliases={}):
    if specs is None:
        specs = [SMEM if a.dtype == jnp.int32 else VMEM for a in args]
    taken = len(args)

    def kernel(*refs):
        body(*refs[:taken], *refs[taken + len(after) :])

    return pl.pallas_call(
        kernel,
        out_shape=outs,
        in_specs=[*specs, *[ANY] * len(after)],
        out_specs=[out] * len(outs),
        scratch_shapes=scratch,
        input_output_aliases=aliases,
        compiler_params=pltpu.CompilerParams(vmem_limit_bytes=limit << 20),
        cost_estimate=cost,
    )(*args, *after)


def hbm(x):
    return pltpu.with_memory_space_constraint(x, pltpu.HBM)


def f32(*shape):
    return jax.ShapeDtypeStruct(shape, jnp.float32)


def position():
    index = lax.axis_index("ang")
    return index // 2 % 2, index % 2


def tile_of(index, group, tiles, core):
    first, half = group
    return index + jnp.where(core == 0, first, tiles - first - half)


def split(x):
    high = x.astype(jnp.bfloat16)
    low = (x - high.astype(jnp.float32)).astype(jnp.bfloat16)
    return high, low


def dot(a, b):
    return jnp.dot(a, b, preferred_element_type=jnp.float32)


def dot_terms(high, low, b):
    both = dot(jnp.concatenate([high, low], axis=0), b)
    return both[: high.shape[0]] + both[high.shape[0] :]


def unrolled(step, count):
    for index in range(count):
        step(index, index % 2)


def paired(step, count):
    def pair(index, carry):
        step(2 * index, 0)
        step(2 * index + 1, 1)
        return carry

    lax.fori_loop(0, count // 2, pair, 0)
    if count % 2:
        step(count - 1, 0)


def resampled_tile(slab_refs, start, weights):
    cols = slab_refs[0].shape[2]
    base = jnp.minimum(start // LANES * LANES, cols - WINDOW)
    columns = pl.ds(pl.multiple_of(base, LANES), WINDOW)
    slabs = [ref[:, :, columns].reshape(-1, WINDOW) for ref in slab_refs]
    slab = jnp.concatenate(slabs, axis=0)
    slab = pltpu.roll(slab, WINDOW - (start - base), 1)[:, : weights.shape[0]]
    return dot_terms(*split(slab), weights)


def resample_own_body(group, start_any, weights_any, sino_any, out_ref, weights_ref, sino_ref, start_ref, sems):
    tiles = weights_any.shape[0]
    held = weights_ref.shape[0]
    first, half = group
    _, core = position()
    place = jnp.where(core == 0, first, held - first - half)
    origin = core * (tiles - held)
    later = jnp.where(core == 0, 0, half)
    needed = [
        pltpu.make_async_copy(start_any, start_ref, sems.at[0]),
        pltpu.make_async_copy(sino_any, sino_ref, sems.at[1]),
        pltpu.make_async_copy(
            weights_any.at[pl.ds(origin + place, half)], weights_ref.at[pl.ds(place, half)], sems.at[2]
        ),
    ]
    rest = pltpu.make_async_copy(
        weights_any.at[pl.ds(origin + later, held - half)],
        weights_ref.at[pl.ds(later, held - half)],
        sems.at[3],
    )
    for copy in (*needed, rest):
        copy.start()
    for copy in needed:
        copy.wait()

    def step(index, slot):
        start = start_ref[origin + place + index]
        out_ref[index] = resampled_tile([sino_ref], start, weights_ref[place + index])

    unrolled(step, half)
    rest.wait()


def resample_own(group, start, weights, sino):
    views, rows, _ = sino.shape
    held = weights.shape[0] // 2
    return call(
        functools.partial(resample_own_body, group),
        [
            f32(group[1], views * rows, LANES),
            jax.ShapeDtypeStruct((held, *weights.shape[1:]), weights.dtype),
            f32(*sino.shape),
        ],
        [pltpu.SMEM(start.shape, jnp.int32), pltpu.SemaphoreType.DMA((4,))],
        [hbm(x) for x in (start, weights, sino)],
        specs=[ANY] * 3,
    )


def resample_rest_body(group, tiles, start_ref, weights_ref, got_ref, done_ref, out_ref):
    held, (first, half) = weights_ref.shape[0], group
    height = done_ref.shape[1]
    _, core = position()
    place = jnp.where(core == 0, first, held - first - half)
    origin = core * (tiles - held)
    mine = pl.multiple_of(core * height, 8)
    other = pl.multiple_of((1 - core) * height, 8)

    def step(index, slot):
        start = start_ref[origin + place + index]
        out_ref[index, pl.ds(mine, height)] = done_ref[index]
        out_ref[index, pl.ds(other, height)] = resampled_tile(
            [got_ref], start, weights_ref[place + index]
        )

    unrolled(step, half)


def resample_rest(group, tiles, start, weights, got, done):
    count, height, _ = done.shape
    return call(
        functools.partial(resample_rest_body, group, tiles),
        [f32(count, 2 * height, LANES)],
        [],
        (start, weights, got, done),
    )[0]


def resample_apart_body(group, tiles, start_ref, weights_ref, sino_ref, got_ref, out_ref, stack):
    held, (first, half) = weights_ref.shape[0], group
    views, rows, _ = sino_ref.shape
    height = views * rows
    _, core = position()
    place = jnp.where(core == 0, first, held - first - half)
    origin = core * (tiles - held)
    mine = pl.multiple_of(core * height, 8)
    other = pl.multiple_of((1 - core) * height, 8)

    def step(index, slot):
        start = start_ref[origin + place + index]
        total = resampled_tile([sino_ref, got_ref], start, weights_ref[place + index])
        stack[slot, pl.ds(mine, height)] = total[:height]
        stack[slot, pl.ds(other, height)] = total[height:]
        for row in range(rows):
            out_ref[index, row] = stack[slot, pl.ds(row, 2 * views, stride=rows), :]

    unrolled(step, half)


def resample_apart(group, tiles, start, weights, sino, got, after):
    views, rows, _ = sino.shape
    return call(
        functools.partial(resample_apart_body, group, tiles),
        [f32(group[1], rows, 2 * views, LANES)],
        [pltpu.VMEM((2, 2 * views * rows + 8, LANES), jnp.float32)],
        (start, weights, sino, got),
        cycles(4000),
        after,
    )[0]


def rows_body(group, held, tiles, offset_ref, odd_ref, even_ref, own_ref, weights_ref, out_ref, stack):
    count, height = out_ref.shape[0], own_ref.shape[1]
    views = height // 2
    _, core = position()
    begin = tile_of(0, group, tiles, core) - tile_of(0, held, tiles, core)
    after = lax.axis_index("row") % 2 == 0
    even_at = pl.multiple_of(jnp.where(after, 2 * height, 0), 8)
    odd_at = pl.multiple_of(jnp.where(after, 0, 2 * height), 8)

    def step(index, slot):
        tile = tile_of(index, group, tiles, core)
        offset = offset_ref[tile]
        stack[slot, pl.ds(even_at, height)] = even_ref[begin + index]
        stack[slot, pl.ds(odd_at, height)] = odd_ref[begin + index]
        stack[slot, height : 2 * height] = own_ref[begin + index]
        weights = weights_ref[:, pl.ds(pl.multiple_of(tile * LANES, LANES), LANES)]

        def picked(row):
            lifted = row + 2
            first = lifted // 2 * height + lifted % 2
            return stack[slot, pl.ds(first, views, stride=2), :]

        terms = [picked(row + offset) for row in range(3)]
        for row in range(2):
            out_ref[index, row] = weights[0:1] * terms[row] + weights[1:2] * terms[row + 1]

    unrolled(step, count)


def interpolate_rows(group, held, tiles, offset, even, odd, own, weights, after, cost):
    height = own.shape[1]
    return call(
        functools.partial(rows_body, group, held, tiles),
        [f32(group[1], 2, height // 2, LANES)],
        [pltpu.VMEM((2, 3 * height + 8, LANES), jnp.float32)],
        (offset, odd, even, own, weights),
        cost,
        after,
    )[0]


def last_rows_body(group, tiles, offset_ref, odd_ref, even_ref, own_ref, weights_ref, keep_ref, send_ref, stack):
    count, parts, rows, chip_views, _ = own_ref.shape
    views = chip_views // 2
    _, core = position()
    after = lax.axis_index("row") % 2 == 0
    even_at = jnp.where(after, 2 * rows, 0)
    odd_at = jnp.where(after, 0, 2 * rows)
    mine = pl.multiple_of(core * views, 8)
    other = pl.multiple_of((1 - core) * views, 8)

    def step(index, slot):
        tile = tile_of(index, group, tiles, core)
        first = offset_ref[tile] + rows
        weights = weights_ref[:, pl.ds(pl.multiple_of(tile * LANES, LANES), LANES)]
        for part in range(parts):
            for row in range(rows):
                stack[slot, even_at + row] = even_ref[index, part, row]
                stack[slot, odd_at + row] = odd_ref[index, part, row]
                stack[slot, rows + row] = own_ref[index, part, row]
            for out_ref, begin in ((keep_ref, mine), (send_ref, other)):
                terms = [stack[slot, first + i, pl.ds(begin, views)] for i in range(rows + 1)]
                for row in range(rows):
                    out_ref[index, part, row] = weights[0:1] * terms[row] + weights[1:2] * terms[row + 1]

    unrolled(step, count)


def interpolate_rows_last(group, tiles, offset, even, odd, own, weights):
    count, parts, rows, chip_views, _ = own.shape
    return call(
        functools.partial(last_rows_body, group, tiles),
        [f32(count, parts, rows, chip_views // 2, LANES)] * 2,
        [pltpu.VMEM((2, 3 * rows, chip_views, LANES), jnp.float32)],
        (offset, odd, even, own, weights),
        cycles(LAST_COST),
    )


def select_body(group, tiles, view_ref, conj_ref, own_ref, got_ref, out_ref):
    count, rows, chip_views, lanes = own_ref.shape
    side, core = position()

    def shifts(index):
        tile = tile_of(index, group, tiles, core)
        shift = view_ref[tile]
        return shift, shift + conj_ref[tiles - 1 - tile]

    def slots(low, high):
        return low + lax.broadcasted_iota(jnp.int32, (high - low, lanes), 0)

    def joined(low, high, first, last):
        if last <= 64:
            return low[first:last]
        if first >= 64:
            return high[first - 64 : last - 64]
        return jnp.concatenate([low[first:64], high[0 : last - 64]], axis=0)

    def across_x(index, row, low, high):
        shift, opposite = shifts(index)
        out = out_ref.at[index, row]
        both = functools.partial(joined, low.at[index, row], high.at[index, row])
        out[0:32] = jnp.where(slots(0, 32) >= shift + 32, both(96, 128), both(0, 32))
        out[32:80] = jnp.where(slots(0, 48) >= opposite + 48, both(16, 64), both(64, 112))
        out[80:88] = jnp.zeros((8, lanes), jnp.float32)

    def across_y_first(index, row, low, high):
        shift, opposite = shifts(index)
        out = out_ref.at[index, row]
        both = functools.partial(joined, low.at[index, row], high.at[index, row])
        out[0:40] = jnp.where(slots(0, 40) >= opposite, both(0, 40), both(72, 112))
        out[40:56] = both(40, 56)
        out[56:72] = jnp.where(slots(56, 72) >= 88 + shift, both(96, 112), both(56, 72))
        out[72:88] = both(112, 128)

    def across_y_last(index, row, low, high):
        shift, opposite = shifts(index)
        out = out_ref.at[index, row]
        both = functools.partial(joined, low.at[index, row], high.at[index, row])
        out[0:16] = both(0, 16)
        out[16:32] = jnp.where(slots(16, 32) < shift + 3, both(16, 32), both(56, 72))
        out[32:48] = both(72, 88)
        out[48:88] = jnp.where(slots(48, 88) < 91 + opposite, both(88, 128), both(16, 56))

    def run(part, low, high):
        for index in range(count):
            for row in range(rows):
                part(index, row, low, high)

    pl.when((core == 0) & (side == 0))(lambda: run(across_x, got_ref, own_ref))
    pl.when((core == 0) & (side == 1))(lambda: run(across_x, own_ref, got_ref))
    pl.when((core == 1) & (side == 0))(lambda: run(across_y_first, own_ref, got_ref))
    pl.when((core == 1) & (side == 1))(lambda: run(across_y_last, got_ref, own_ref))


def select_views(group, tiles, view_offset, conj_offset, own, got, after=(), cost=SHORT):
    count, rows, chip_views, _ = own.shape
    return call(
        functools.partial(select_body, group, tiles),
        [f32(count, rows, SLOTS, LANES)],
        [],
        (view_offset, conj_offset, own, got),
        cost,
        after,
    )[0]


def views_body(group, tiles, exchanged, view_ref, conj_ref, weights_ref, *refs):
    *blocks, stack = refs
    outs = blocks[3 if exchanged else 6 :]
    blocks = blocks[: 3 if exchanged else 6]
    count, _, rows, views, _ = outs[0].shape
    side, core = position()
    firsts = (core, 1 - core) if len(outs) == 2 else (0,)
    taps = weights_ref.shape[0]

    def interpolate(index, slot, row):
        tile = tile_of(index, group, tiles, core)
        weights = weights_ref[:, pl.ds(pl.multiple_of(tile * LANES, LANES), LANES)]
        shift = view_ref[tile]
        opposite = shift + conj_ref[tiles - 1 - tile]
        for part, by in ((0, 32 + shift), (1, 176 + opposite)):
            for out_ref, first in zip(outs, firsts):
                begin = by + first * views
                total = weights[0:1] * stack[slot, row, pl.ds(begin, views)]
                for tap in range(1, taps):
                    total = total + weights[tap : tap + 1] * stack[slot, row, pl.ds(begin + tap, views)]
                out_ref[index, part, row] = total

    def run(parts):
        def step(index, slot):
            for row in range(rows):
                at = 0
                for part in parts(*(ref.at[index, row] for ref in blocks)):
                    stack[slot, row, at : at + part.shape[0]] = part[...]
                    at += part.shape[0]
                interpolate(index, slot, row)

        unrolled(step, count)

    def from_neighbours(before, own, after, early, middle, late):
        return before, own, after, early, middle, late

    def from_x(own, beyond, got):
        near, far = got.at[0:32], got.at[32:80]
        return near, own, near, far, beyond, far

    def from_y_first(own, beside, got):
        return got.at[56:88], own, beside.at[0:32], beside.at[16:64], got.at[0:72], got.at[0:40]

    def from_y_last(own, beside, got):
        return beside.at[32:64], own, got.at[0:32], got.at[48:88], got.at[16:88], beside.at[0:48]

    if exchanged:
        pl.when(core == 0)(lambda: run(from_x))
        pl.when((core == 1) & (side == 0))(lambda: run(from_y_first))
        pl.when((core == 1) & (side == 1))(lambda: run(from_y_last))
    else:
        run(from_neighbours)


def interpolate_views(group, tiles, exchanged, view_offset, conj_offset, weights, blocks, pieces, cost=SHORT, after=()):
    count, rows, chip_views, _ = blocks[0 if exchanged else 1].shape
    return call(
        functools.partial(views_body, group, tiles, exchanged),
        [f32(count, 2, rows, chip_views // pieces, LANES)] * pieces,
        [pltpu.VMEM((2, rows, 288, LANES), jnp.float32)],
        (view_offset, conj_offset, weights, *blocks),
        cost,
        after,
    )


def ramp(lag):
    lag = lag.astype(np.float64)
    odd = np.abs(lag) % 2 == 1
    values = np.where(lag == 0, 0.25, np.where(odd, -1.0 / (math.pi**2 * np.maximum(lag * lag, 1.0)), 0.0))
    return np.where(np.abs(lag) <= KR, values, 0.0).astype(np.float32)


def filter_matrix():
    column = np.arange(WINDOW)[:, None]
    place = np.arange(2 * LANES)[None, :]
    lag = place - 2 * (column - LANES)
    whole = np.concatenate([ramp(lag), ramp(lag - 1)[::-1]], axis=0)
    high = whole.astype(jnp.bfloat16)
    low = (whole - high.astype(np.float32)).astype(jnp.bfloat16)
    return jnp.asarray(high), jnp.asarray(low)


def stage_spans(groups, number, tiles):
    first, half = groups[number]
    begin = first - 1 if number else 0
    if number == len(groups) - 1:
        ranges = [(begin, tiles - begin)]
    else:
        ranges = [(begin, first + half - 1), (tiles - first - half + 1, tiles - begin)]
    spans = []
    for low, high in ranges:
        while low < high:
            count = min(4, high - low)
            spans.append((low, count))
            low += count
    return spans


def filter_body(groups, held, number, tiles, high_ref, low_ref, *refs):
    parts = refs[: 2 * len(held)]
    if number:
        earlier, out_any, mixed, high_all, low_all, result, sems = refs[2 * len(held) :]
    else:
        result, mixed, high_all, low_all = refs[2:]
    views = result.shape[0]
    _, core = position()
    if number == 0:
        for ref in (high_all, low_all):
            for part in range(2):
                ref[part, 0] = jnp.zeros(ref.shape[2:], ref.dtype)
                ref[part, tiles + 1] = jnp.zeros(ref.shape[2:], ref.dtype)

    def gather(group, ref, owner, index, slot):
        tile = tile_of(index, group, tiles, owner)
        for part in range(2):
            for row in range(2):
                mixed[slot, part, pl.ds(row, views, stride=2), :] = ref[index, part, row]
            high, low = split(mixed[slot, part, 0 : 2 * views])
            high_all[part, tile + 1] = high
            low_all[part, tile + 1] = low

    for place, group in enumerate(held):
        pair = parts[2 * place : 2 * place + 2]
        for ref, owner in zip(pair, (core, 1 - core)):
            if group[0] >= groups[number][0]:
                unrolled(functools.partial(gather, group, ref, owner), group[1])
                continue
            begin = jnp.where(owner == 0, group[1] - 2, 0)
            for i in range(2):
                gather(group, ref, owner, begin + i, i)

    copies = []

    def leave(source, first, count):
        columns = pl.ds(first * 2 * LANES, count * 2 * LANES)
        copies.append(
            pltpu.make_async_copy(source.at[:, :, columns], out_any.at[:, :, columns], sems.at[len(copies)])
        )
        copies[-1].start()

    if number:
        for first, count in stage_spans(groups, 0, tiles):
            leave(earlier, first, count)
    for first, count in stage_spans(groups, number, tiles):

        def window(ref):
            pieces = []
            for section in range(3):
                piece = ref[0, first + section : first + section + count]
                pieces.append(piece.reshape(count * 2 * views, LANES))
            for section in range(3):
                last = tiles - 1 - first + section
                piece = jnp.stack([ref[1, last - i] for i in range(count)])
                pieces.append(piece.reshape(count * 2 * views, LANES))
            return jnp.concatenate(pieces, axis=1)

        high, low = window(high_all), window(low_all)
        total = dot_terms(high, low, high_ref[...]) + dot(high, low_ref[...])
        for i in range(count):
            block = total[2 * views * i : 2 * views * (i + 1)].reshape(views, 2, 2 * LANES)
            result[:, :, (first + i) * 2 * LANES : (first + i + 1) * 2 * LANES] = block
        if number:
            leave(result, first, count)
    for copy in copies:
        copy.wait()


def ramp_filter(groups, held, number, tiles, keeps, gots, out):
    views = keeps[0].shape[3]
    args = [*filter_matrix()]
    for keep, got in zip(keeps, gots):
        args += [keep, got]
    stored = pltpu.VMEM((2, tiles + 2, 2 * views, LANES), jnp.bfloat16)
    scratch = [pltpu.VMEM((2, 2, 2 * views + 8, LANES), jnp.float32), stored, stored]
    shape = f32(views, 2, 2 * tiles * LANES)
    if number:
        args.append(out)
        spans = sum(len(stage_spans(groups, i, tiles)) for i in range(2))
        scratch += [pltpu.VMEM(shape.shape, jnp.float32), pltpu.SemaphoreType.DMA((spans,))]
    return call(
        functools.partial(filter_body, groups, held, number, tiles),
        [shape],
        scratch,
        args,
        out=ANY if number else VMEM,
        cost=SHORT if number else cycles(6000),
    )[0]


def permuted(value, axis, target):
    count = lax.axis_size(axis)
    pairs = [(i, target(i)) for i in range(count)]
    return lax.ppermute(value, axis, [(i, j) for i, j in pairs if 0 <= j < count])


def swapped(value):
    return permuted(value, "ang", lambda i: i ^ 1)


def row_pairs(own):
    even = permuted(own, "row", lambda i: i ^ 1)
    odd = permuted(own, "row", lambda i: ((i + 1) ^ 1) - 1)
    return even, odd


def first_exchange(own):
    if lax.axis_size("ang") == 8:
        return [permuted(own, "ang", lambda i: i ^ (2 if i % 2 else 4))]
    return []


def second_exchange(own, first, chosen):
    devices = lax.axis_size("ang")
    if first:
        return [own, *first, permuted(chosen[0], "ang", lambda i: i ^ (4 if i % 2 else 2))]

    def ahead(begin, end, chips):
        return permuted(own[:, :, begin:end], "ang", lambda i: (i - 2 * chips) % devices)

    turned = devices // 4
    return [
        ahead(32, 64, -1),
        own,
        ahead(0, 32, 1),
        ahead(16, 64, turned - 1),
        ahead(0, 64, turned),
        ahead(0, 48, turned + 1),
    ]


def on_device(
    sinogram, col_weights, col_start, view_offset, row_offset, conj_offset, ang_weights, row_weights
):
    tiles = col_weights.shape[0]
    exchanged = lax.axis_size("ang") == 8
    offsets = (view_offset, conj_offset)
    outer, *others = GROUPS
    inner = (others[0][0], sum(half for _, half in others))

    beside = swapped(sinogram)
    own, weights, sino = resample_own(inner, col_start, col_weights, sinogram)
    resampled = resample_rest(inner, tiles, col_start, weights, beside, own)
    halo = row_pairs(resampled)
    block = resample_apart(outer, tiles, col_start, weights, sino, beside, (resampled,))

    first = first_exchange(block)
    chosen = [select_views(outer, tiles, *offsets, block, got) for got in first]
    parts = second_exchange(block, first, chosen)
    blocks = [
        interpolate_rows(group, inner, tiles, row_offset, *halo, resampled, row_weights, chosen, cost)
        for group, cost in zip(others, (cycles(10000), cycles(1)))
    ]
    (whole,) = interpolate_views(
        outer, tiles, exchanged, *offsets, ang_weights, parts, 1, cycles(1), tuple(blocks)
    )
    outer_halo = row_pairs(whole)
    keep, send = interpolate_rows_last(outer, tiles, row_offset, *outer_halo, whole, row_weights)
    keeps, gots = [keep], [swapped(send)]

    for group, block, cost in zip(others, blocks, (SHORT, cycles(8000))):
        first = first_exchange(block)
        selected = [select_views(group, tiles, *offsets, block, got, (whole,), cost) for got in first]
        parts = second_exchange(block, first, selected)
        keep, send = interpolate_views(group, tiles, exchanged, *offsets, ang_weights, parts, 2)
        keeps.append(keep)
        gots.append(swapped(send))
    stages = (outer, inner)
    out = ramp_filter(stages, GROUPS[:1], 0, tiles, keeps[:1], gots[:1], None)
    return ramp_filter(stages, GROUPS, 1, tiles, keeps, gots, out)


def solution(mesh):
    return jax.shard_map(
        on_device,
        mesh=mesh,
        in_specs=(P("ang", "row", None), P(), P(), P(), P(), P(), P(), P()),
        out_specs=P("ang", "row", None),
        check_vma=False,
    )
```

```python
import functools
import math

import jax
import jax.numpy as jnp
import numpy as np
from jax import lax
from jax.experimental import pallas as pl
from jax.experimental.pallas import tpu as pltpu
from jax.sharding import PartitionSpec as P

KR = 256
LAST_COST = 1
GROUPS = ((0, 5), (5, 6), (11, 5))
LANES = 128
WINDOW = 3 * LANES
SLOTS = 88
VMEM = pl.BlockSpec(memory_space=pltpu.VMEM)
SMEM = pl.BlockSpec(memory_space=pltpu.SMEM)
ANY = pl.BlockSpec(memory_space=pl.ANY)
SHORT = pl.CostEstimate(flops=1, bytes_accessed=1, transcendentals=0)


def cycles(number):
    return pl.CostEstimate(flops=number << 19, bytes_accessed=1, transcendentals=0)


def call(body, outs, scratch, args, cost=SHORT, after=(), specs=None, limit=48, out=VMEM, aliases={}):
    if specs is None:
        specs = [SMEM if a.dtype == jnp.int32 else VMEM for a in args]
    taken = len(args)

    def kernel(*refs):
        body(*refs[:taken], *refs[taken + len(after) :])

    return pl.pallas_call(
        kernel,
        out_shape=outs,
        in_specs=[*specs, *[ANY] * len(after)],
        out_specs=[out] * len(outs),
        scratch_shapes=scratch,
        input_output_aliases=aliases,
        compiler_params=pltpu.CompilerParams(vmem_limit_bytes=limit << 20),
        cost_estimate=cost,
    )(*args, *after)


def hbm(x):
    return pltpu.with_memory_space_constraint(x, pltpu.HBM)


def f32(*shape):
    return jax.ShapeDtypeStruct(shape, jnp.float32)


def position():
    index = lax.axis_index("ang")
    return index // 2 % 2, index % 2


def tile_of(index, group, tiles, core):
    first, half = group
    return index + jnp.where(core == 0, first, tiles - first - half)


def split(x):
    high = x.astype(jnp.bfloat16)
    low = (x - high.astype(jnp.float32)).astype(jnp.bfloat16)
    return high, low


def dot(a, b):
    return jnp.dot(a, b, preferred_element_type=jnp.float32)


def dot_terms(high, low, b):
    both = dot(jnp.concatenate([high, low], axis=0), b)
    return both[: high.shape[0]] + both[high.shape[0] :]


def unrolled(step, count):
    for index in range(count):
        step(index, index % 2)


def paired(step, count):
    def pair(index, carry):
        step(2 * index, 0)
        step(2 * index + 1, 1)
        return carry

    lax.fori_loop(0, count // 2, pair, 0)
    if count % 2:
        step(count - 1, 0)


def resampled_tile(slab_refs, start, weights):
    cols = slab_refs[0].shape[2]
    base = jnp.minimum(start // LANES * LANES, cols - WINDOW)
    columns = pl.ds(pl.multiple_of(base, LANES), WINDOW)
    slabs = [ref[:, :, columns].reshape(-1, WINDOW) for ref in slab_refs]
    slab = jnp.concatenate(slabs, axis=0)
    slab = pltpu.roll(slab, WINDOW - (start - base), 1)[:, : weights.shape[0]]
    return dot_terms(*split(slab), weights)


def resample_own_body(group, start_any, weights_any, sino_any, out_ref, weights_ref, sino_ref, start_ref, sems):
    tiles = weights_any.shape[0]
    held = weights_ref.shape[0]
    first, half = group
    _, core = position()
    place = jnp.where(core == 0, first, held - first - half)
    origin = core * (tiles - held)
    later = jnp.where(core == 0, 0, half)
    needed = [
        pltpu.make_async_copy(start_any, start_ref, sems.at[0]),
        pltpu.make_async_copy(sino_any, sino_ref, sems.at[1]),
        pltpu.make_async_copy(
            weights_any.at[pl.ds(origin + place, half)], weights_ref.at[pl.ds(place, half)], sems.at[2]
        ),
    ]
    rest = pltpu.make_async_copy(
        weights_any.at[pl.ds(origin + later, held - half)],
        weights_ref.at[pl.ds(later, held - half)],
        sems.at[3],
    )
    for copy in (*needed, rest):
        copy.start()
    for copy in needed:
        copy.wait()

    def step(index, slot):
        start = start_ref[origin + place + index]
        out_ref[index] = resampled_tile([sino_ref], start, weights_ref[place + index])

    unrolled(step, half)
    rest.wait()


def resample_own(group, start, weights, sino):
    views, rows, _ = sino.shape
    held = weights.shape[0] // 2
    return call(
        functools.partial(resample_own_body, group),
        [
            f32(group[1], views * rows, LANES),
            jax.ShapeDtypeStruct((held, *weights.shape[1:]), weights.dtype),
            f32(*sino.shape),
        ],
        [pltpu.SMEM(start.shape, jnp.int32), pltpu.SemaphoreType.DMA((4,))],
        [hbm(x) for x in (start, weights, sino)],
        specs=[ANY] * 3,
    )


def resample_rest_body(group, tiles, start_ref, weights_ref, got_ref, done_ref, out_ref):
    held, (first, half) = weights_ref.shape[0], group
    height = done_ref.shape[1]
    _, core = position()
    place = jnp.where(core == 0, first, held - first - half)
    origin = core * (tiles - held)
    mine = pl.multiple_of(core * height, 8)
    other = pl.multiple_of((1 - core) * height, 8)

    def step(index, slot):
        start = start_ref[origin + place + index]
        out_ref[index, pl.ds(mine, height)] = done_ref[index]
        out_ref[index, pl.ds(other, height)] = resampled_tile(
            [got_ref], start, weights_ref[place + index]
        )

    unrolled(step, half)


def resample_rest(group, tiles, start, weights, got, done):
    count, height, _ = done.shape
    return call(
        functools.partial(resample_rest_body, group, tiles),
        [f32(count, 2 * height, LANES)],
        [],
        (start, weights, got, done),
    )[0]


def resample_apart_body(group, tiles, start_ref, weights_ref, sino_ref, got_ref, out_ref, stack):
    held, (first, half) = weights_ref.shape[0], group
    views, rows, _ = sino_ref.shape
    height = views * rows
    _, core = position()
    place = jnp.where(core == 0, first, held - first - half)
    origin = core * (tiles - held)
    mine = pl.multiple_of(core * height, 8)
    other = pl.multiple_of((1 - core) * height, 8)

    def step(index, slot):
        start = start_ref[origin + place + index]
        total = resampled_tile([sino_ref, got_ref], start, weights_ref[place + index])
        stack[slot, pl.ds(mine, height)] = total[:height]
        stack[slot, pl.ds(other, height)] = total[height:]
        for row in range(rows):
            out_ref[index, row] = stack[slot, pl.ds(row, 2 * views, stride=rows), :]

    unrolled(step, half)


def resample_apart(group, tiles, start, weights, sino, got, after):
    views, rows, _ = sino.shape
    return call(
        functools.partial(resample_apart_body, group, tiles),
        [f32(group[1], rows, 2 * views, LANES)],
        [pltpu.VMEM((2, 2 * views * rows + 8, LANES), jnp.float32)],
        (start, weights, sino, got),
        cycles(4000),
        after,
    )[0]


def rows_body(group, held, tiles, offset_ref, odd_ref, even_ref, own_ref, weights_ref, out_ref):
    count, height = out_ref.shape[0], own_ref.shape[1]
    views = height // 2
    _, core = position()
    begin = tile_of(0, group, tiles, core) - tile_of(0, held, tiles, core)

    def run(before, after):
        def step(index, slot):
            tile = tile_of(index, group, tiles, core)
            offset = offset_ref[tile]
            weights = weights_ref[:, pl.ds(pl.multiple_of(tile * LANES, LANES), LANES)]
            lines = [
                ref[begin + index, pl.ds(row, views, stride=2), :]
                for ref in (before, own_ref, after)
                for row in range(2)
            ]
            terms = []
            for row in range(3):
                low = jnp.where(offset == -2, lines[row], lines[row + 1])
                high = jnp.where(offset == 0, lines[row + 2], lines[row + 3])
                terms.append(jnp.where(offset < 0, low, high))
            for row in range(2):
                out_ref[index, row] = weights[0:1] * terms[row] + weights[1:2] * terms[row + 1]

        unrolled(step, count)

    beside = lax.axis_index("row") % 2
    pl.when(beside == 0)(lambda: run(odd_ref, even_ref))
    pl.when(beside == 1)(lambda: run(even_ref, odd_ref))


def interpolate_rows(group, held, tiles, offset, even, odd, own, weights, after, cost):
    height = own.shape[1]
    return call(
        functools.partial(rows_body, group, held, tiles),
        [f32(group[1], 2, height // 2, LANES)],
        [],
        (offset, odd, even, own, weights),
        cost,
        after,
    )[0]


def last_rows_body(group, tiles, offset_ref, odd_ref, even_ref, own_ref, weights_ref, keep_ref, send_ref, stack):
    count, parts, rows, chip_views, _ = own_ref.shape
    views = chip_views // 2
    _, core = position()
    after = lax.axis_index("row") % 2 == 0
    even_at = jnp.where(after, 2 * rows, 0)
    odd_at = jnp.where(after, 0, 2 * rows)
    mine = pl.multiple_of(core * views, 8)
    other = pl.multiple_of((1 - core) * views, 8)

    def step(index, slot):
        tile = tile_of(index, group, tiles, core)
        first = offset_ref[tile] + rows
        weights = weights_ref[:, pl.ds(pl.multiple_of(tile * LANES, LANES), LANES)]
        for part in range(parts):
            for row in range(rows):
                stack[slot, even_at + row] = even_ref[index, part, row]
                stack[slot, odd_at + row] = odd_ref[index, part, row]
                stack[slot, rows + row] = own_ref[index, part, row]
            for out_ref, begin in ((keep_ref, mine), (send_ref, other)):
                terms = [stack[slot, first + i, pl.ds(begin, views)] for i in range(rows + 1)]
                for row in range(rows):
                    out_ref[index, part, row] = weights[0:1] * terms[row] + weights[1:2] * terms[row + 1]

    unrolled(step, count)


def interpolate_rows_last(group, tiles, offset, even, odd, own, weights):
    count, parts, rows, chip_views, _ = own.shape
    return call(
        functools.partial(last_rows_body, group, tiles),
        [f32(count, parts, rows, chip_views // 2, LANES)] * 2,
        [pltpu.VMEM((2, 3 * rows, chip_views, LANES), jnp.float32)],
        (offset, odd, even, own, weights),
        cycles(LAST_COST),
    )


def select_body(group, tiles, view_ref, conj_ref, own_ref, got_ref, out_ref):
    count, rows, chip_views, lanes = own_ref.shape
    side, core = position()

    def shifts(index):
        tile = tile_of(index, group, tiles, core)
        shift = view_ref[tile]
        return shift, shift + conj_ref[tiles - 1 - tile]

    def slots(low, high):
        return low + lax.broadcasted_iota(jnp.int32, (high - low, lanes), 0)

    def joined(low, high, first, last):
        if last <= 64:
            return low[first:last]
        if first >= 64:
            return high[first - 64 : last - 64]
        return jnp.concatenate([low[first:64], high[0 : last - 64]], axis=0)

    def across_x(index, row, low, high):
        shift, opposite = shifts(index)
        out = out_ref.at[index, row]
        both = functools.partial(joined, low.at[index, row], high.at[index, row])
        out[0:32] = jnp.where(slots(0, 32) >= shift + 32, both(96, 128), both(0, 32))
        out[32:80] = jnp.where(slots(0, 48) >= opposite + 48, both(16, 64), both(64, 112))
        out[80:88] = jnp.zeros((8, lanes), jnp.float32)

    def across_y_first(index, row, low, high):
        shift, opposite = shifts(index)
        out = out_ref.at[index, row]
        both = functools.partial(joined, low.at[index, row], high.at[index, row])
        out[0:40] = jnp.where(slots(0, 40) >= opposite, both(0, 40), both(72, 112))
        out[40:56] = both(40, 56)
        out[56:72] = jnp.where(slots(56, 72) >= 88 + shift, both(96, 112), both(56, 72))
        out[72:88] = both(112, 128)

    def across_y_last(index, row, low, high):
        shift, opposite = shifts(index)
        out = out_ref.at[index, row]
        both = functools.partial(joined, low.at[index, row], high.at[index, row])
        out[0:16] = both(0, 16)
        out[16:32] = jnp.where(slots(16, 32) < shift + 3, both(16, 32), both(56, 72))
        out[32:48] = both(72, 88)
        out[48:88] = jnp.where(slots(48, 88) < 91 + opposite, both(88, 128), both(16, 56))

    def run(part, low, high):
        for index in range(count):
            for row in range(rows):
                part(index, row, low, high)

    pl.when((core == 0) & (side == 0))(lambda: run(across_x, got_ref, own_ref))
    pl.when((core == 0) & (side == 1))(lambda: run(across_x, own_ref, got_ref))
    pl.when((core == 1) & (side == 0))(lambda: run(across_y_first, own_ref, got_ref))
    pl.when((core == 1) & (side == 1))(lambda: run(across_y_last, got_ref, own_ref))


def select_views(group, tiles, view_offset, conj_offset, own, got, after=(), cost=SHORT):
    count, rows, chip_views, _ = own.shape
    return call(
        functools.partial(select_body, group, tiles),
        [f32(count, rows, SLOTS, LANES)],
        [],
        (view_offset, conj_offset, own, got),
        cost,
        after,
    )[0]


def views_body(group, tiles, exchanged, view_ref, conj_ref, weights_ref, *refs):
    *blocks, stack = refs
    outs = blocks[3 if exchanged else 6 :]
    blocks = blocks[: 3 if exchanged else 6]
    count, _, rows, views, _ = outs[0].shape
    side, core = position()
    firsts = (core, 1 - core) if len(outs) == 2 else (0,)
    taps = weights_ref.shape[0]

    def interpolate(index, slot, row):
        tile = tile_of(index, group, tiles, core)
        weights = weights_ref[:, pl.ds(pl.multiple_of(tile * LANES, LANES), LANES)]
        shift = view_ref[tile]
        opposite = shift + conj_ref[tiles - 1 - tile]
        for part, by in ((0, 32 + shift), (1, 176 + opposite)):
            for out_ref, first in zip(outs, firsts):
                begin = by + first * views
                total = weights[0:1] * stack[slot, row, pl.ds(begin, views)]
                for tap in range(1, taps):
                    total = total + weights[tap : tap + 1] * stack[slot, row, pl.ds(begin + tap, views)]
                out_ref[index, part, row] = total

    def run(parts):
        def step(index, slot):
            for row in range(rows):
                at = 0
                for part in parts(*(ref.at[index, row] for ref in blocks)):
                    stack[slot, row, at : at + part.shape[0]] = part[...]
                    at += part.shape[0]
                interpolate(index, slot, row)

        unrolled(step, count)

    def from_neighbours(before, own, after, early, middle, late):
        return before, own, after, early, middle, late

    def from_x(own, beyond, got):
        near, far = got.at[0:32], got.at[32:80]
        return near, own, near, far, beyond, far

    def from_y_first(own, beside, got):
        return got.at[56:88], own, beside.at[0:32], beside.at[16:64], got.at[0:72], got.at[0:40]

    def from_y_last(own, beside, got):
        return beside.at[32:64], own, got.at[0:32], got.at[48:88], got.at[16:88], beside.at[0:48]

    if exchanged:
        pl.when(core == 0)(lambda: run(from_x))
        pl.when((core == 1) & (side == 0))(lambda: run(from_y_first))
        pl.when((core == 1) & (side == 1))(lambda: run(from_y_last))
    else:
        run(from_neighbours)


def interpolate_views(group, tiles, exchanged, view_offset, conj_offset, weights, blocks, pieces, cost=SHORT, after=()):
    count, rows, chip_views, _ = blocks[0 if exchanged else 1].shape
    return call(
        functools.partial(views_body, group, tiles, exchanged),
        [f32(count, 2, rows, chip_views // pieces, LANES)] * pieces,
        [pltpu.VMEM((2, rows, 288, LANES), jnp.float32)],
        (view_offset, conj_offset, weights, *blocks),
        cost,
        after,
    )


def ramp(lag):
    lag = lag.astype(np.float64)
    odd = np.abs(lag) % 2 == 1
    values = np.where(lag == 0, 0.25, np.where(odd, -1.0 / (math.pi**2 * np.maximum(lag * lag, 1.0)), 0.0))
    return np.where(np.abs(lag) <= KR, values, 0.0).astype(np.float32)


def filter_matrix():
    column = np.arange(WINDOW)[:, None]
    place = np.arange(2 * LANES)[None, :]
    lag = place - 2 * (column - LANES)
    whole = np.concatenate([ramp(lag), ramp(lag - 1)[::-1]], axis=0)
    high = whole.astype(jnp.bfloat16)
    low = (whole - high.astype(np.float32)).astype(jnp.bfloat16)
    return jnp.asarray(high), jnp.asarray(low)


def stage_spans(groups, number, tiles):
    first, half = groups[number]
    begin = first - 1 if number else 0
    if number == len(groups) - 1:
        ranges = [(begin, tiles - begin)]
    else:
        ranges = [(begin, first + half - 1), (tiles - first - half + 1, tiles - begin)]
    spans = []
    for low, high in ranges:
        while low < high:
            count = min(4, high - low)
            spans.append((low, count))
            low += count
    return spans


def filter_body(groups, held, number, tiles, high_ref, low_ref, *refs):
    parts = refs[: 2 * len(held)]
    if number:
        earlier, out_any, mixed, high_all, low_all, result, sems = refs[2 * len(held) :]
    else:
        result, mixed, high_all, low_all = refs[2:]
    views = result.shape[0]
    _, core = position()
    if number == 0:
        for ref in (high_all, low_all):
            for part in range(2):
                ref[part, 0] = jnp.zeros(ref.shape[2:], ref.dtype)
                ref[part, tiles + 1] = jnp.zeros(ref.shape[2:], ref.dtype)

    def gather(group, ref, owner, index, slot):
        tile = tile_of(index, group, tiles, owner)
        for part in range(2):
            for row in range(2):
                mixed[slot, part, pl.ds(row, views, stride=2), :] = ref[index, part, row]
            high, low = split(mixed[slot, part, 0 : 2 * views])
            high_all[part, tile + 1] = high
            low_all[part, tile + 1] = low

    for place, group in enumerate(held):
        pair = parts[2 * place : 2 * place + 2]
        for ref, owner in zip(pair, (core, 1 - core)):
            if group[0] >= groups[number][0]:
                unrolled(functools.partial(gather, group, ref, owner), group[1])
                continue
            begin = jnp.where(owner == 0, group[1] - 2, 0)
            for i in range(2):
                gather(group, ref, owner, begin + i, i)

    copies = []

    def leave(source, first, count):
        columns = pl.ds(first * 2 * LANES, count * 2 * LANES)
        copies.append(
            pltpu.make_async_copy(source.at[:, :, columns], out_any.at[:, :, columns], sems.at[len(copies)])
        )
        copies[-1].start()

    if number:
        for first, count in stage_spans(groups, 0, tiles):
            leave(earlier, first, count)
    for first, count in stage_spans(groups, number, tiles):

        def window(ref):
            pieces = []
            for section in range(3):
                piece = ref[0, first + section : first + section + count]
                pieces.append(piece.reshape(count * 2 * views, LANES))
            for section in range(3):
                last = tiles - 1 - first + section
                piece = jnp.stack([ref[1, last - i] for i in range(count)])
                pieces.append(piece.reshape(count * 2 * views, LANES))
            return jnp.concatenate(pieces, axis=1)

        high, low = window(high_all), window(low_all)
        total = dot_terms(high, low, high_ref[...]) + dot(high, low_ref[...])
        for i in range(count):
            block = total[2 * views * i : 2 * views * (i + 1)].reshape(views, 2, 2 * LANES)
            result[:, :, (first + i) * 2 * LANES : (first + i + 1) * 2 * LANES] = block
        if number:
            leave(result, first, count)
    for copy in copies:
        copy.wait()


def ramp_filter(groups, held, number, tiles, keeps, gots, out):
    views = keeps[0].shape[3]
    args = [*filter_matrix()]
    for keep, got in zip(keeps, gots):
        args += [keep, got]
    stored = pltpu.VMEM((2, tiles + 2, 2 * views, LANES), jnp.bfloat16)
    scratch = [pltpu.VMEM((2, 2, 2 * views + 8, LANES), jnp.float32), stored, stored]
    shape = f32(views, 2, 2 * tiles * LANES)
    if number:
        args.append(out)
        spans = sum(len(stage_spans(groups, i, tiles)) for i in range(2))
        scratch += [pltpu.VMEM(shape.shape, jnp.float32), pltpu.SemaphoreType.DMA((spans,))]
    return call(
        functools.partial(filter_body, groups, held, number, tiles),
        [shape],
        scratch,
        args,
        out=ANY if number else VMEM,
        cost=SHORT if number else cycles(3000),
    )[0]


def permuted(value, axis, target):
    count = lax.axis_size(axis)
    pairs = [(i, target(i)) for i in range(count)]
    return lax.ppermute(value, axis, [(i, j) for i, j in pairs if 0 <= j < count])


def swapped(value):
    return permuted(value, "ang", lambda i: i ^ 1)


def row_pairs(own):
    even = permuted(own, "row", lambda i: i ^ 1)
    odd = permuted(own, "row", lambda i: ((i + 1) ^ 1) - 1)
    return even, odd


def first_exchange(own):
    if lax.axis_size("ang") == 8:
        return [permuted(own, "ang", lambda i: i ^ (2 if i % 2 else 4))]
    return []


def second_exchange(own, first, chosen):
    devices = lax.axis_size("ang")
    if first:
        return [own, *first, permuted(chosen[0], "ang", lambda i: i ^ (4 if i % 2 else 2))]

    def ahead(begin, end, chips):
        return permuted(own[:, :, begin:end], "ang", lambda i: (i - 2 * chips) % devices)

    turned = devices // 4
    return [
        ahead(32, 64, -1),
        own,
        ahead(0, 32, 1),
        ahead(16, 64, turned - 1),
        ahead(0, 64, turned),
        ahead(0, 48, turned + 1),
    ]


def on_device(
    sinogram, col_weights, col_start, view_offset, row_offset, conj_offset, ang_weights, row_weights
):
    tiles = col_weights.shape[0]
    exchanged = lax.axis_size("ang") == 8
    offsets = (view_offset, conj_offset)
    outer, *others = GROUPS
    inner = (others[0][0], sum(half for _, half in others))

    beside = swapped(sinogram)
    own, weights, sino = resample_own(inner, col_start, col_weights, sinogram)
    resampled = resample_rest(inner, tiles, col_start, weights, beside, own)
    halo = row_pairs(resampled)
    block = resample_apart(outer, tiles, col_start, weights, sino, beside, (resampled,))

    first = first_exchange(block)
    chosen = [select_views(outer, tiles, *offsets, block, got) for got in first]
    parts = second_exchange(block, first, chosen)
    blocks = [
        interpolate_rows(group, inner, tiles, row_offset, *halo, resampled, row_weights, chosen, cost)
        for group, cost in zip(others, (cycles(10000), cycles(1)))
    ]
    (whole,) = interpolate_views(
        outer, tiles, exchanged, *offsets, ang_weights, parts, 1, cycles(1), tuple(blocks)
    )
    outer_halo = row_pairs(whole)
    keep, send = interpolate_rows_last(outer, tiles, row_offset, *outer_halo, whole, row_weights)
    keeps, gots = [keep], [swapped(send)]

    for group, block, cost in zip(others, blocks, (SHORT, cycles(8000))):
        first = first_exchange(block)
        selected = [select_views(group, tiles, *offsets, block, got, (whole,), cost) for got in first]
        parts = second_exchange(block, first, selected)
        keep, send = interpolate_views(group, tiles, exchanged, *offsets, ang_weights, parts, 2)
        keeps.append(keep)
        gots.append(swapped(send))
    stages = (outer, inner)
    out = ramp_filter(stages, GROUPS[:1], 0, tiles, keeps[:1], gots[:1], None)
    return ramp_filter(stages, GROUPS, 1, tiles, keeps, gots, out)


def solution(mesh):
    return jax.shard_map(
        on_device,
        mesh=mesh,
        in_specs=(P("ang", "row", None), P(), P(), P(), P(), P(), P(), P()),
        out_specs=P("ang", "row", None),
        check_vma=False,
    )
```

```python
import functools
import math

import jax
import jax.numpy as jnp
import numpy as np
from jax import lax
from jax.experimental import pallas as pl
from jax.experimental.pallas import tpu as pltpu
from jax.sharding import PartitionSpec as P

KR = 256
LAST_COST = 1
GROUPS = ((0, 5), (5, 5), (10, 6))
LANES = 128
WINDOW = 3 * LANES
SLOTS = 88
VMEM = pl.BlockSpec(memory_space=pltpu.VMEM)
SMEM = pl.BlockSpec(memory_space=pltpu.SMEM)
ANY = pl.BlockSpec(memory_space=pl.ANY)
SHORT = pl.CostEstimate(flops=1, bytes_accessed=1, transcendentals=0)


def cycles(number):
    return pl.CostEstimate(flops=number << 19, bytes_accessed=1, transcendentals=0)


def call(body, outs, scratch, args, cost=SHORT, after=(), specs=None, limit=48, out=VMEM, aliases={}):
    if specs is None:
        specs = [SMEM if a.dtype == jnp.int32 else VMEM for a in args]
    taken = len(args)

    def kernel(*refs):
        body(*refs[:taken], *refs[taken + len(after) :])

    return pl.pallas_call(
        kernel,
        out_shape=outs,
        in_specs=[*specs, *[ANY] * len(after)],
        out_specs=[out] * len(outs),
        scratch_shapes=scratch,
        input_output_aliases=aliases,
        compiler_params=pltpu.CompilerParams(vmem_limit_bytes=limit << 20),
        cost_estimate=cost,
    )(*args, *after)


def hbm(x):
    return pltpu.with_memory_space_constraint(x, pltpu.HBM)


def f32(*shape):
    return jax.ShapeDtypeStruct(shape, jnp.float32)


def position():
    index = lax.axis_index("ang")
    return index // 2 % 2, index % 2


def tile_of(index, group, tiles, core):
    first, half = group
    return index + jnp.where(core == 0, first, tiles - first - half)


def split(x):
    high = x.astype(jnp.bfloat16)
    low = (x - high.astype(jnp.float32)).astype(jnp.bfloat16)
    return high, low


def dot(a, b):
    return jnp.dot(a, b, preferred_element_type=jnp.float32)


def dot_terms(high, low, b):
    both = dot(jnp.concatenate([high, low], axis=0), b)
    return both[: high.shape[0]] + both[high.shape[0] :]


def unrolled(step, count):
    for index in range(count):
        step(index, index % 2)


def paired(step, count):
    def pair(index, carry):
        step(2 * index, 0)
        step(2 * index + 1, 1)
        return carry

    lax.fori_loop(0, count // 2, pair, 0)
    if count % 2:
        step(count - 1, 0)


def resampled_tile(slab_refs, start, weights):
    cols = slab_refs[0].shape[2]
    base = jnp.minimum(start // LANES * LANES, cols - WINDOW)
    columns = pl.ds(pl.multiple_of(base, LANES), WINDOW)
    slabs = [ref[:, :, columns].reshape(-1, WINDOW) for ref in slab_refs]
    slab = jnp.concatenate(slabs, axis=0)
    slab = pltpu.roll(slab, WINDOW - (start - base), 1)[:, : weights.shape[0]]
    return dot_terms(*split(slab), weights)


def resample_own_body(group, start_any, weights_any, sino_any, out_ref, weights_ref, sino_ref, start_ref, sems):
    tiles = weights_any.shape[0]
    held = weights_ref.shape[0]
    first, half = group
    _, core = position()
    place = jnp.where(core == 0, first, held - first - half)
    origin = core * (tiles - held)
    later = jnp.where(core == 0, 0, half)
    needed = [
        pltpu.make_async_copy(start_any, start_ref, sems.at[0]),
        pltpu.make_async_copy(sino_any, sino_ref, sems.at[1]),
        pltpu.make_async_copy(
            weights_any.at[pl.ds(origin + place, half)], weights_ref.at[pl.ds(place, half)], sems.at[2]
        ),
    ]
    rest = pltpu.make_async_copy(
        weights_any.at[pl.ds(origin + later, held - half)],
        weights_ref.at[pl.ds(later, held - half)],
        sems.at[3],
    )
    for copy in (*needed, rest):
        copy.start()
    for copy in needed:
        copy.wait()

    def step(index, slot):
        start = start_ref[origin + place + index]
        out_ref[index] = resampled_tile([sino_ref], start, weights_ref[place + index])

    unrolled(step, half)
    rest.wait()


def resample_own(group, start, weights, sino):
    views, rows, _ = sino.shape
    held = weights.shape[0] // 2
    return call(
        functools.partial(resample_own_body, group),
        [
            f32(group[1], views * rows, LANES),
            jax.ShapeDtypeStruct((held, *weights.shape[1:]), weights.dtype),
            f32(*sino.shape),
        ],
        [pltpu.SMEM(start.shape, jnp.int32), pltpu.SemaphoreType.DMA((4,))],
        [hbm(x) for x in (start, weights, sino)],
        specs=[ANY] * 3,
    )


def resample_rest_body(group, tiles, start_ref, weights_ref, got_ref, done_ref, out_ref):
    held, (first, half) = weights_ref.shape[0], group
    height = done_ref.shape[1]
    _, core = position()
    place = jnp.where(core == 0, first, held - first - half)
    origin = core * (tiles - held)
    mine = pl.multiple_of(core * height, 8)
    other = pl.multiple_of((1 - core) * height, 8)

    def step(index, slot):
        start = start_ref[origin + place + index]
        out_ref[index, pl.ds(mine, height)] = done_ref[index]
        out_ref[index, pl.ds(other, height)] = resampled_tile(
            [got_ref], start, weights_ref[place + index]
        )

    unrolled(step, half)


def resample_rest(group, tiles, start, weights, got, done):
    count, height, _ = done.shape
    return call(
        functools.partial(resample_rest_body, group, tiles),
        [f32(count, 2 * height, LANES)],
        [],
        (start, weights, got, done),
    )[0]


def resample_apart_body(group, tiles, start_ref, weights_ref, sino_ref, got_ref, out_ref, stack):
    held, (first, half) = weights_ref.shape[0], group
    views, rows, _ = sino_ref.shape
    height = views * rows
    _, core = position()
    place = jnp.where(core == 0, first, held - first - half)
    origin = core * (tiles - held)
    mine = pl.multiple_of(core * height, 8)
    other = pl.multiple_of((1 - core) * height, 8)

    def step(index, slot):
        start = start_ref[origin + place + index]
        total = resampled_tile([sino_ref, got_ref], start, weights_ref[place + index])
        stack[slot, pl.ds(mine, height)] = total[:height]
        stack[slot, pl.ds(other, height)] = total[height:]
        for row in range(rows):
            out_ref[index, row] = stack[slot, pl.ds(row, 2 * views, stride=rows), :]

    unrolled(step, half)


def resample_apart(group, tiles, start, weights, sino, got, after):
    views, rows, _ = sino.shape
    return call(
        functools.partial(resample_apart_body, group, tiles),
        [f32(group[1], rows, 2 * views, LANES)],
        [pltpu.VMEM((2, 2 * views * rows + 8, LANES), jnp.float32)],
        (start, weights, sino, got),
        cycles(4000),
        after,
    )[0]


def rows_body(group, held, tiles, offset_ref, odd_ref, even_ref, own_ref, weights_ref, out_ref):
    count, height = out_ref.shape[0], own_ref.shape[1]
    views = height // 2
    _, core = position()
    begin = tile_of(0, group, tiles, core) - tile_of(0, held, tiles, core)

    def run(before, after):
        def step(index, slot):
            tile = tile_of(index, group, tiles, core)
            offset = offset_ref[tile]
            weights = weights_ref[:, pl.ds(pl.multiple_of(tile * LANES, LANES), LANES)]
            lines = [
                ref[begin + index, pl.ds(row, views, stride=2), :]
                for ref in (before, own_ref, after)
                for row in range(2)
            ]
            terms = []
            for row in range(3):
                low = jnp.where(offset == -2, lines[row], lines[row + 1])
                high = jnp.where(offset == 0, lines[row + 2], lines[row + 3])
                terms.append(jnp.where(offset < 0, low, high))
            for row in range(2):
                out_ref[index, row] = weights[0:1] * terms[row] + weights[1:2] * terms[row + 1]

        unrolled(step, count)

    beside = lax.axis_index("row") % 2
    pl.when(beside == 0)(lambda: run(odd_ref, even_ref))
    pl.when(beside == 1)(lambda: run(even_ref, odd_ref))


def interpolate_rows(group, held, tiles, offset, even, odd, own, weights, after, cost):
    height = own.shape[1]
    return call(
        functools.partial(rows_body, group, held, tiles),
        [f32(group[1], 2, height // 2, LANES)],
        [],
        (offset, odd, even, own, weights),
        cost,
        after,
    )[0]


def last_rows_body(group, tiles, offset_ref, odd_ref, even_ref, own_ref, weights_ref, keep_ref, send_ref, stack):
    count, parts, rows, chip_views, _ = own_ref.shape
    views = chip_views // 2
    _, core = position()
    after = lax.axis_index("row") % 2 == 0
    even_at = jnp.where(after, 2 * rows, 0)
    odd_at = jnp.where(after, 0, 2 * rows)
    mine = pl.multiple_of(core * views, 8)
    other = pl.multiple_of((1 - core) * views, 8)

    def step(index, slot):
        tile = tile_of(index, group, tiles, core)
        first = offset_ref[tile] + rows
        weights = weights_ref[:, pl.ds(pl.multiple_of(tile * LANES, LANES), LANES)]
        for part in range(parts):
            for row in range(rows):
                stack[slot, even_at + row] = even_ref[index, part, row]
                stack[slot, odd_at + row] = odd_ref[index, part, row]
                stack[slot, rows + row] = own_ref[index, part, row]
            for out_ref, begin in ((keep_ref, mine), (send_ref, other)):
                terms = [stack[slot, first + i, pl.ds(begin, views)] for i in range(rows + 1)]
                for row in range(rows):
                    out_ref[index, part, row] = weights[0:1] * terms[row] + weights[1:2] * terms[row + 1]

    unrolled(step, count)


def interpolate_rows_last(group, tiles, offset, even, odd, own, weights):
    count, parts, rows, chip_views, _ = own.shape
    return call(
        functools.partial(last_rows_body, group, tiles),
        [f32(count, parts, rows, chip_views // 2, LANES)] * 2,
        [pltpu.VMEM((2, 3 * rows, chip_views, LANES), jnp.float32)],
        (offset, odd, even, own, weights),
        cycles(LAST_COST),
    )


def select_body(group, tiles, view_ref, conj_ref, own_ref, got_ref, out_ref):
    count, rows, chip_views, lanes = own_ref.shape
    side, core = position()

    def shifts(index):
        tile = tile_of(index, group, tiles, core)
        shift = view_ref[tile]
        return shift, shift + conj_ref[tiles - 1 - tile]

    def slots(low, high):
        return low + lax.broadcasted_iota(jnp.int32, (high - low, lanes), 0)

    def joined(low, high, first, last):
        if last <= 64:
            return low[first:last]
        if first >= 64:
            return high[first - 64 : last - 64]
        return jnp.concatenate([low[first:64], high[0 : last - 64]], axis=0)

    def across_x(index, row, low, high):
        shift, opposite = shifts(index)
        out = out_ref.at[index, row]
        both = functools.partial(joined, low.at[index, row], high.at[index, row])
        out[0:32] = jnp.where(slots(0, 32) >= shift + 32, both(96, 128), both(0, 32))
        out[32:80] = jnp.where(slots(0, 48) >= opposite + 48, both(16, 64), both(64, 112))
        out[80:88] = jnp.zeros((8, lanes), jnp.float32)

    def across_y_first(index, row, low, high):
        shift, opposite = shifts(index)
        out = out_ref.at[index, row]
        both = functools.partial(joined, low.at[index, row], high.at[index, row])
        out[0:40] = jnp.where(slots(0, 40) >= opposite, both(0, 40), both(72, 112))
        out[40:56] = both(40, 56)
        out[56:72] = jnp.where(slots(56, 72) >= 88 + shift, both(96, 112), both(56, 72))
        out[72:88] = both(112, 128)

    def across_y_last(index, row, low, high):
        shift, opposite = shifts(index)
        out = out_ref.at[index, row]
        both = functools.partial(joined, low.at[index, row], high.at[index, row])
        out[0:16] = both(0, 16)
        out[16:32] = jnp.where(slots(16, 32) < shift + 3, both(16, 32), both(56, 72))
        out[32:48] = both(72, 88)
        out[48:88] = jnp.where(slots(48, 88) < 91 + opposite, both(88, 128), both(16, 56))

    def run(part, low, high):
        for index in range(count):
            for row in range(rows):
                part(index, row, low, high)

    pl.when((core == 0) & (side == 0))(lambda: run(across_x, got_ref, own_ref))
    pl.when((core == 0) & (side == 1))(lambda: run(across_x, own_ref, got_ref))
    pl.when((core == 1) & (side == 0))(lambda: run(across_y_first, own_ref, got_ref))
    pl.when((core == 1) & (side == 1))(lambda: run(across_y_last, got_ref, own_ref))


def select_views(group, tiles, view_offset, conj_offset, own, got, after=(), cost=SHORT):
    count, rows, chip_views, _ = own.shape
    return call(
        functools.partial(select_body, group, tiles),
        [f32(count, rows, SLOTS, LANES)],
        [],
        (view_offset, conj_offset, own, got),
        cost,
        after,
    )[0]


def views_body(group, tiles, exchanged, view_ref, conj_ref, weights_ref, *refs):
    *blocks, stack = refs
    outs = blocks[3 if exchanged else 6 :]
    blocks = blocks[: 3 if exchanged else 6]
    count, _, rows, views, _ = outs[0].shape
    side, core = position()
    firsts = (core, 1 - core) if len(outs) == 2 else (0,)
    taps = weights_ref.shape[0]

    def interpolate(index, slot, row):
        tile = tile_of(index, group, tiles, core)
        weights = weights_ref[:, pl.ds(pl.multiple_of(tile * LANES, LANES), LANES)]
        shift = view_ref[tile]
        opposite = shift + conj_ref[tiles - 1 - tile]
        for part, by in ((0, 32 + shift), (1, 176 + opposite)):
            for out_ref, first in zip(outs, firsts):
                begin = by + first * views
                total = weights[0:1] * stack[slot, row, pl.ds(begin, views)]
                for tap in range(1, taps):
                    total = total + weights[tap : tap + 1] * stack[slot, row, pl.ds(begin + tap, views)]
                out_ref[index, part, row] = total

    def run(parts):
        def step(index, slot):
            for row in range(rows):
                at = 0
                for part in parts(*(ref.at[index, row] for ref in blocks)):
                    stack[slot, row, at : at + part.shape[0]] = part[...]
                    at += part.shape[0]
                interpolate(index, slot, row)

        unrolled(step, count)

    def from_neighbours(before, own, after, early, middle, late):
        return before, own, after, early, middle, late

    def from_x(own, beyond, got):
        near, far = got.at[0:32], got.at[32:80]
        return near, own, near, far, beyond, far

    def from_y_first(own, beside, got):
        return got.at[56:88], own, beside.at[0:32], beside.at[16:64], got.at[0:72], got.at[0:40]

    def from_y_last(own, beside, got):
        return beside.at[32:64], own, got.at[0:32], got.at[48:88], got.at[16:88], beside.at[0:48]

    if exchanged:
        pl.when(core == 0)(lambda: run(from_x))
        pl.when((core == 1) & (side == 0))(lambda: run(from_y_first))
        pl.when((core == 1) & (side == 1))(lambda: run(from_y_last))
    else:
        run(from_neighbours)


def interpolate_views(group, tiles, exchanged, view_offset, conj_offset, weights, blocks, pieces, cost=SHORT, after=()):
    count, rows, chip_views, _ = blocks[0 if exchanged else 1].shape
    return call(
        functools.partial(views_body, group, tiles, exchanged),
        [f32(count, 2, rows, chip_views // pieces, LANES)] * pieces,
        [pltpu.VMEM((2, rows, 288, LANES), jnp.float32)],
        (view_offset, conj_offset, weights, *blocks),
        cost,
        after,
    )


def ramp(lag):
    lag = lag.astype(np.float64)
    odd = np.abs(lag) % 2 == 1
    values = np.where(lag == 0, 0.25, np.where(odd, -1.0 / (math.pi**2 * np.maximum(lag * lag, 1.0)), 0.0))
    return np.where(np.abs(lag) <= KR, values, 0.0).astype(np.float32)


def filter_matrix():
    column = np.arange(WINDOW)[:, None]
    place = np.arange(2 * LANES)[None, :]
    lag = place - 2 * (column - LANES)
    whole = np.concatenate([ramp(lag), ramp(lag - 1)[::-1]], axis=0)
    high = whole.astype(jnp.bfloat16)
    low = (whole - high.astype(np.float32)).astype(jnp.bfloat16)
    return jnp.asarray(high), jnp.asarray(low)


def stage_spans(groups, number, tiles):
    first, half = groups[number]
    begin = first - 1 if number else 0
    if number == len(groups) - 1:
        ranges = [(begin, tiles - begin)]
    else:
        ranges = [(begin, first + half - 1), (tiles - first - half + 1, tiles - begin)]
    spans = []
    for low, high in ranges:
        while low < high:
            count = min(4, high - low)
            spans.append((low, count))
            low += count
    return spans


def filter_body(groups, held, number, tiles, high_ref, low_ref, *refs):
    parts = refs[: 2 * len(held)]
    if number:
        earlier, out_any, mixed, high_all, low_all, result, sems = refs[2 * len(held) :]
    else:
        result, mixed, high_all, low_all = refs[2:]
    views = result.shape[0]
    _, core = position()
    if number == 0:
        for ref in (high_all, low_all):
            for part in range(2):
                ref[part, 0] = jnp.zeros(ref.shape[2:], ref.dtype)
                ref[part, tiles + 1] = jnp.zeros(ref.shape[2:], ref.dtype)

    def gather(group, ref, owner, index, slot):
        tile = tile_of(index, group, tiles, owner)
        for part in range(2):
            for row in range(2):
                mixed[slot, part, pl.ds(row, views, stride=2), :] = ref[index, part, row]
            high, low = split(mixed[slot, part, 0 : 2 * views])
            high_all[part, tile + 1] = high
            low_all[part, tile + 1] = low

    for place, group in enumerate(held):
        pair = parts[2 * place : 2 * place + 2]
        for ref, owner in zip(pair, (core, 1 - core)):
            if group[0] >= groups[number][0]:
                unrolled(functools.partial(gather, group, ref, owner), group[1])
                continue
            begin = jnp.where(owner == 0, group[1] - 2, 0)
            for i in range(2):
                gather(group, ref, owner, begin + i, i)

    copies = []

    def leave(source, first, count):
        columns = pl.ds(first * 2 * LANES, count * 2 * LANES)
        copies.append(
            pltpu.make_async_copy(source.at[:, :, columns], out_any.at[:, :, columns], sems.at[len(copies)])
        )
        copies[-1].start()

    if number:
        for first, count in stage_spans(groups, 0, tiles):
            leave(earlier, first, count)
    for first, count in stage_spans(groups, number, tiles):

        def window(ref):
            pieces = []
            for section in range(3):
                piece = ref[0, first + section : first + section + count]
                pieces.append(piece.reshape(count * 2 * views, LANES))
            for section in range(3):
                last = tiles - 1 - first + section
                piece = jnp.stack([ref[1, last - i] for i in range(count)])
                pieces.append(piece.reshape(count * 2 * views, LANES))
            return jnp.concatenate(pieces, axis=1)

        high, low = window(high_all), window(low_all)
        total = dot_terms(high, low, high_ref[...]) + dot(high, low_ref[...])
        for i in range(count):
            block = total[2 * views * i : 2 * views * (i + 1)].reshape(views, 2, 2 * LANES)
            result[:, :, (first + i) * 2 * LANES : (first + i + 1) * 2 * LANES] = block
        if number:
            leave(result, first, count)
    for copy in copies:
        copy.wait()


def ramp_filter(groups, held, number, tiles, keeps, gots, out):
    views = keeps[0].shape[3]
    args = [*filter_matrix()]
    for keep, got in zip(keeps, gots):
        args += [keep, got]
    stored = pltpu.VMEM((2, tiles + 2, 2 * views, LANES), jnp.bfloat16)
    scratch = [pltpu.VMEM((2, 2, 2 * views + 8, LANES), jnp.float32), stored, stored]
    shape = f32(views, 2, 2 * tiles * LANES)
    if number:
        args.append(out)
        spans = sum(len(stage_spans(groups, i, tiles)) for i in range(2))
        scratch += [pltpu.VMEM(shape.shape, jnp.float32), pltpu.SemaphoreType.DMA((spans,))]
    return call(
        functools.partial(filter_body, groups, held, number, tiles),
        [shape],
        scratch,
        args,
        out=ANY if number else VMEM,
        cost=SHORT if number else cycles(3000),
    )[0]


def permuted(value, axis, target):
    count = lax.axis_size(axis)
    pairs = [(i, target(i)) for i in range(count)]
    return lax.ppermute(value, axis, [(i, j) for i, j in pairs if 0 <= j < count])


def swapped(value):
    return permuted(value, "ang", lambda i: i ^ 1)


def row_pairs(own):
    even = permuted(own, "row", lambda i: i ^ 1)
    odd = permuted(own, "row", lambda i: ((i + 1) ^ 1) - 1)
    return even, odd


def first_exchange(own):
    if lax.axis_size("ang") == 8:
        return [permuted(own, "ang", lambda i: i ^ (2 if i % 2 else 4))]
    return []


def second_exchange(own, first, chosen):
    devices = lax.axis_size("ang")
    if first:
        return [own, *first, permuted(chosen[0], "ang", lambda i: i ^ (4 if i % 2 else 2))]

    def ahead(begin, end, chips):
        return permuted(own[:, :, begin:end], "ang", lambda i: (i - 2 * chips) % devices)

    turned = devices // 4
    return [
        ahead(32, 64, -1),
        own,
        ahead(0, 32, 1),
        ahead(16, 64, turned - 1),
        ahead(0, 64, turned),
        ahead(0, 48, turned + 1),
    ]


def on_device(
    sinogram, col_weights, col_start, view_offset, row_offset, conj_offset, ang_weights, row_weights
):
    tiles = col_weights.shape[0]
    exchanged = lax.axis_size("ang") == 8
    offsets = (view_offset, conj_offset)
    outer, *others = GROUPS
    inner = (others[0][0], sum(half for _, half in others))

    beside = swapped(sinogram)
    own, weights, sino = resample_own(inner, col_start, col_weights, sinogram)
    resampled = resample_rest(inner, tiles, col_start, weights, beside, own)
    halo = row_pairs(resampled)
    block = resample_apart(outer, tiles, col_start, weights, sino, beside, (resampled,))

    first = first_exchange(block)
    chosen = [select_views(outer, tiles, *offsets, block, got) for got in first]
    parts = second_exchange(block, first, chosen)
    blocks = [
        interpolate_rows(group, inner, tiles, row_offset, *halo, resampled, row_weights, chosen, cost)
        for group, cost in zip(others, (cycles(10000), cycles(1)))
    ]
    (whole,) = interpolate_views(
        outer, tiles, exchanged, *offsets, ang_weights, parts, 1, cycles(1), tuple(blocks)
    )
    outer_halo = row_pairs(whole)
    keep, send = interpolate_rows_last(outer, tiles, row_offset, *outer_halo, whole, row_weights)
    keeps, gots = [keep], [swapped(send)]

    for group, block, cost in zip(others, blocks, (SHORT, cycles(8000))):
        first = first_exchange(block)
        selected = [select_views(group, tiles, *offsets, block, got, (whole,), cost) for got in first]
        parts = second_exchange(block, first, selected)
        keep, send = interpolate_views(group, tiles, exchanged, *offsets, ang_weights, parts, 2)
        keeps.append(keep)
        gots.append(swapped(send))
    stages = (outer, inner)
    out = ramp_filter(stages, GROUPS[:1], 0, tiles, keeps[:1], gots[:1], None)
    return ramp_filter(stages, GROUPS, 1, tiles, keeps, gots, out)


def solution(mesh):
    return jax.shard_map(
        on_device,
        mesh=mesh,
        in_specs=(P("ang", "row", None), P(), P(), P(), P(), P(), P(), P()),
        out_specs=P("ang", "row", None),
        check_vma=False,
    )
```
